32 devices in a mesh: row: 4 (over y, x), col: 8 (over z, core).
Axes of the slice: x: 2, y: 2, z: 4, core: 2. Of those that a mesh axis runs over, the one named last changes fastest.
Arguments:
- amplitudes: bfloat16 [8000, 2800], P('row', 'col'), may hold values from -6 to 6
- values_stored: bfloat16 [2800, 11200], P('row', 'col'), may hold values from -0.109375 to 0.109375
- irrep_virtual: int32 [1400], replicated, may hold values from 0 to 7
- residual_in: float32 [8000, 11200], P('row', 'col'), may hold values from -6 to 6
Outputs:
- residual_out: float32 [8000, 11200], P('row', 'col')
The draws below stay inside these ranges and needn't reach their ends.
Inputs may be any that keep to these rules, and one draw needn't show every extreme that they name: `irrep_virtual`: labels of the eight irreducible representations of D2h.
All inputs are finite; a program needn't handle non-finite values.
Results may differ from the reference program's by a relative error of at most 0.0003.
Values may be sent and summed in bfloat16 or wider, within the bound.
No kernel may reach another device: no remote copies, remote signals or barrier semaphores. Data moves between devices by JAX's collectives and lax.ppermute only.
A program may use at most 128 MiB of HBM per device.

```python
import jax
import jax.numpy as jnp
from jax import lax

NVIR = 1400
C_SLAB = 2
OCC_PAIRS = 8000
SLAB_PAIRS = 2800
VIR_PAIRS = 11200


def with_ends(array, key, least, largest):
    longest = array.shape.index(max(array.shape))
    spots = []
    for shift in (0, 1):
        where = [jax.random.randint(jax.random.fold_in(key, axis), (), 0, length) for axis, length in enumerate(array.shape)]
        where[longest] = (where[longest] + shift) % array.shape[longest]
        spots.append(tuple(where))
    return array.at[spots[0]].set(least).at[spots[1]].set(largest)


def steps_of(key, extent, split, least, high):
    factor_of = 1.0
    for axis_at, shards_of in split:
        steps = jax.random.uniform(jax.random.fold_in(jax.random.fold_in(key, 6), axis_at), (shards_of,), jnp.float32, least / len(split), high / len(split))
        factor_of = factor_of * jnp.repeat(jnp.exp(steps), extent[axis_at] // shards_of).reshape((-1,) + (1,) * (len(extent) - 1 - axis_at))
    return factor_of


def centred(key, shape, spread, reach, pieces=(), kind=jnp.bfloat16):
    drawn = jax.random.normal(key, shape, jnp.float32) * spread
    if len(pieces) > 0:
        drawn = steps_of(key, shape, pieces, -0.22, 0.18) * drawn
    return jnp.clip(drawn, min=-reach, max=reach).astype(kind)


def setup_inputs(seed: int = 0) -> dict:
    splits = jax.random.split(jax.random.key(seed), 5)
    return {
        "amplitudes": centred(splits[0], (OCC_PAIRS, SLAB_PAIRS), 1.0, 6.0, ((0, 4), (1, 8))),
        "values_stored": centred(splits[1], (SLAB_PAIRS, VIR_PAIRS), SLAB_PAIRS ** -0.5, 0.109375, ((0, 4), (1, 8))),
        "irrep_virtual": with_ends(jax.random.randint(splits[2], (NVIR,), 0, 8), jax.random.fold_in(splits[2], 1), 0, 7).astype(jnp.int32),
        "residual_in": centred(splits[3], (OCC_PAIRS, VIR_PAIRS), 1.0, 6.0, ((0, 4), (1, 8)), jnp.float32),
    }


def stored_order(irrep_virtual):
    pair_irrep = jnp.bitwise_xor(irrep_virtual[:C_SLAB][:, None], irrep_virtual[None, :]).reshape(-1)
    count_pairs = pair_irrep.shape[0]
    sort_key = pair_irrep * count_pairs + jnp.arange(count_pairs, dtype=jnp.int32)
    return jnp.argsort(sort_key).astype(jnp.int32)


def reference(amplitudes, values_stored, irrep_virtual, residual_in):
    stored = stored_order(irrep_virtual)
    sorted_columns = jnp.take(amplitudes, stored, axis=1).astype(jnp.float32)
    product = jnp.dot(sorted_columns, values_stored.astype(jnp.float32), precision=lax.Precision.HIGHEST)
    return residual_in + product
```

```python
import functools

import jax
import jax.numpy as jnp
import numpy as np
from jax import lax
from jax.experimental import pallas as pl
from jax.experimental.pallas import tpu as pltpu
from jax.sharding import PartitionSpec as P

C_SLAB = 2
CORES = 2
TILE = 256
CHUNKS = (4, 4)
CONTRACT_FIRST = (((0,), (0,)), ((), ()))


def round_up(value, step):
    return -(-value // step) * step


def stored_positions(irrep_virtual, chips, depth, depth_padded):
    pair_irrep = jnp.bitwise_xor(irrep_virtual[:C_SLAB][:, None], irrep_virtual[None, :]).reshape(-1)
    count = pair_irrep.shape[0]
    key = pair_irrep * count + jnp.arange(count, dtype=jnp.int32)
    blocks = jnp.pad(
        key.reshape(chips * CORES, depth), ((0, 0), (0, depth_padded - depth)), constant_values=-1
    ).reshape(chips, CORES * depth_padded, 1)
    rank = jnp.sum((key[None, None, :] < blocks).astype(jnp.int32), axis=2, keepdims=True)
    return jnp.where(blocks < 0, -1, rank)


def permute_kernel(count, has_previous, base_ref, pos_ref, *refs):
    out_ref = refs[-1]
    total = refs[count][0].astype(jnp.float32) if has_previous else None
    pos = pos_ref[0]
    for s in range(count):
        rows = refs[s].shape[0]
        picks = pos - base_ref[s] == lax.broadcasted_iota(jnp.int32, (pos.shape[0], rows), 1)
        term = jnp.dot(picks.astype(jnp.bfloat16), refs[s][...], preferred_element_type=jnp.float32)
        total = term if total is None else total + term
    out_ref[0] = total.astype(out_ref.dtype)


def add_permuted(pos, parts, bases, previous):
    chips, rows, _ = pos.shape
    columns = parts[0].shape[1]
    block = pl.BlockSpec((1, rows, columns), lambda q, *_: (q, 0, 0))
    in_specs = [pl.BlockSpec((1, rows, 1), lambda q, *_: (q, 0, 0))]
    in_specs += [
        pl.BlockSpec(part.shape, lambda q, *_: (0, 0), pipeline_mode=pl.Buffered(1)) for part in parts
    ]
    operands = [jnp.stack(bases).astype(jnp.int32), pos, *parts]
    aliases = {}
    if previous is not None:
        in_specs.append(block)
        aliases = {len(operands): 0}
        operands.append(previous)
    return pl.pallas_call(
        functools.partial(permute_kernel, len(parts), previous is not None),
        grid_spec=pltpu.PrefetchScalarGridSpec(
            num_scalar_prefetch=1, grid=(chips,), in_specs=in_specs, out_specs=block
        ),
        out_shape=jax.ShapeDtypeStruct((chips, rows, columns), parts[0].dtype),
        input_output_aliases=aliases,
        compiler_params=pltpu.CompilerParams(vmem_limit_bytes=32 << 20),
        cost_estimate=pl.CostEstimate(
            flops=2 * chips * rows * columns * sum(part.shape[0] for part in parts),
            bytes_accessed=4 * chips * rows * columns,
            transcendentals=0,
        ),
    )(*operands)


def gather_integrals(values, size):
    half = round_up(values.shape[0] // 2, 16)

    def send(array, bit):
        return lax.ppermute(array, "row", [(i, i ^ bit) for i in range(size)])

    got = {0: [values]}
    order = sorted(range(1, size), key=lambda d: (bin(d).count("1"), d))
    for d in order:
        low, high = d & -d, 1 << (d.bit_length() - 1)
        if low == high:
            got[d] = [send(values, d)]
            continue
        parts = []
        for which, bit in ((0, low), (1, high)):
            source = got[d ^ bit]
            if len(source) == 2:
                piece = source[which]
            else:
                piece = source[0][:half] if which == 0 else source[0][half:]
            parts.append(send(piece, bit))
        got[d] = parts
    return got, order, half


def slot_table(chips):
    table = []
    for z in range(chips):
        line = []
        for s in range(1, chips):
            if z + s < chips:
                line.append((("L", s), z + s))
            if z - s >= 0:
                line.append((("R", s), z - s))
        table.append(line)
    return table


def spread_line(chunk, chips):
    got = {}
    swap_all = [(i, i ^ 1) for i in range(chips * CORES)]
    got["own", 0] = (chunk, lax.ppermute(chunk, "col", swap_all))
    held = {"L": chunk, "R": chunk}
    for s in range(1, chips):
        for way, step in (("L", -1), ("R", 1)):
            pairs = []
            ends = []
            for z in range(chips):
                source = z + s if step < 0 else z - s
                if 0 <= source < chips:
                    ends.append(z)
                    for core in range(CORES):
                        pairs.append(((z - step) * CORES + core, z * CORES + core))
            held[way] = lax.ppermute(held[way], "col", pairs)
            swap = [(z * CORES + core, z * CORES + 1 - core) for z in ends for core in range(CORES)]
            got[way, s] = (held[way], lax.ppermute(held[way], "col", swap))
    return got


def product_kernel(slots, chunk_tiles, depth, info_ref, *refs):
    count = len(slots)
    offsets = np.cumsum([0, *slots])
    n_arrays = int(offsets[-1]) * len(chunk_tiles) * CORES
    arrays = refs[:n_arrays]
    natural_ref, acc_ref = refs[n_arrays], refs[n_arrays + 1]
    out_ref, buffer, integrals, sems, sem_integrals = refs[n_arrays + 2 :]
    core = info_ref[0]
    tile = acc_ref.shape[0]
    i = pl.program_id(0)
    steps = sum(chunk_tiles)

    def fetch(step, slot_of_buffer):
        first = 0
        for h, tiles in enumerate(chunk_tiles):

            @pl.when(jnp.logical_and(step >= first, step < first + tiles))
            def _(h=h, first=first):
                lanes = pl.ds(pl.multiple_of((step - first) * tile, tile), tile)
                for s in range(count):
                    for k in range(slots[s]):
                        at = ((int(offsets[s]) + k) * len(chunk_tiles) + h) * CORES

                        def start(at=at, s=s):
                            for other in range(CORES):
                                place = jnp.where(core == other, 0, depth) + 2 * depth * s
                                pltpu.make_async_copy(
                                    arrays[at + other].at[:, lanes],
                                    buffer.at[slot_of_buffer, pl.ds(pl.multiple_of(place, 16), depth), :],
                                    sems.at[slot_of_buffer],
                                ).start()

                        if slots[s] == 1:
                            start()
                        else:
                            pl.when(info_ref[1 + s] == k)(start)

            first += tiles

    @pl.when(i == 0)
    def _():
        for s in range(count):
            pltpu.make_async_copy(
                natural_ref.at[info_ref[1 + count + s]],
                integrals.at[pl.ds(2 * depth * s, 2 * depth), :],
                sem_integrals,
            ).start()
        fetch(0, 0)

    @pl.when(i + 1 < steps)
    def _():
        fetch(i + 1, lax.rem(i + 1, 2))

    @pl.when(i == 0)
    def _():
        pltpu.make_async_copy(integrals, integrals, sem_integrals).wait()

    now = lax.rem(i, 2)
    pltpu.make_async_copy(buffer.at[now], buffer.at[now], sems.at[now]).wait()
    out_ref[...] = acc_ref[...] + lax.dot_general(
        buffer[now], integrals[...], CONTRACT_FIRST, preferred_element_type=jnp.float32
    )


def add_product(info, slots, natural, acc, first_tile, in_place):
    tile = TILE
    chunk_tiles = tuple(pair[0].shape[1] // tile for pair in slots[0][0])
    depth = slots[0][0][0][0].shape[0]
    columns = natural.shape[2]
    arrays = [a for slot in slots for candidate in slot for pair in candidate for a in pair]
    anywhere = pl.BlockSpec(memory_space=pl.ANY)
    block = pl.BlockSpec((tile, columns), lambda i, *_: (first_tile + i, 0))
    operands = [info, *arrays, natural, acc]
    rows = 2 * depth * len(slots)
    lanes = sum(chunk_tiles) * tile
    return pl.pallas_call(
        functools.partial(product_kernel, tuple(len(slot) for slot in slots), chunk_tiles, depth),
        grid_spec=pltpu.PrefetchScalarGridSpec(
            num_scalar_prefetch=1,
            grid=(sum(chunk_tiles),),
            in_specs=[anywhere] * (len(arrays) + 1) + [block],
            out_specs=block,
            scratch_shapes=[
                pltpu.VMEM((2, rows, tile), natural.dtype),
                pltpu.VMEM((rows, columns), natural.dtype),
                pltpu.SemaphoreType.DMA((2,)),
                pltpu.SemaphoreType.DMA,
            ],
        ),
        out_shape=jax.ShapeDtypeStruct(acc.shape, acc.dtype),
        input_output_aliases={len(operands) - 1: 0} if in_place else {},
        compiler_params=pltpu.CompilerParams(vmem_limit_bytes=32 << 20),
        cost_estimate=pl.CostEstimate(
            flops=2 * lanes * rows * columns,
            bytes_accessed=8 * lanes * columns + 2 * rows * (lanes + columns),
            transcendentals=0,
        ),
    )(*operands)


def on_device(chips, row_size, amplitudes, values_stored, irrep_virtual, residual_in):
    occ, depth = amplitudes.shape
    depth_padded = round_up(depth, 16)
    chip = lax.axis_index("col") // CORES
    core = lax.axis_index("col") % CORES
    row = lax.axis_index("row")

    lanes = sum(CHUNKS) * TILE
    columns_first = jnp.pad(amplitudes.T, ((0, depth_padded - depth), (0, lanes - occ)))
    edges = np.cumsum([0, *CHUNKS]) * TILE
    chunks = [columns_first[:, edges[h] : edges[h + 1]] for h in range(len(CHUNKS))]

    spread = [spread_line(chunk, chips) for chunk in chunks]
    got, order, half = gather_integrals(values_stored, row_size)

    pos = stored_positions(irrep_virtual, chips, depth, depth_padded)
    stored_rows = values_stored.shape[0]
    natural = add_permuted(pos, [values_stored], [row * stored_rows], None)
    single = [d for d in order if len(got[d]) == 1]
    natural = add_permuted(pos, [got[d][0] for d in single], [(row ^ d) * stored_rows for d in single], natural)
    for d in order:
        if len(got[d]) == 2:
            base = (row ^ d) * stored_rows
            natural = add_permuted(pos, got[d], [base, base + half], natural)

    table = slot_table(chips)
    slots, choices, sources = [[("own", 0)]], [jnp.int32(0)], [chip]
    for t in range(chips - 1):
        candidates = sorted({table[z][t][0] for z in range(chips)})
        slots.append(candidates)
        choices.append(jnp.asarray([candidates.index(table[z][t][0]) for z in range(chips)], jnp.int32)[chip])
        sources.append(jnp.asarray([table[z][t][1] for z in range(chips)], jnp.int32)[chip])

    def info_of(which):
        return jnp.stack([core, *[choices[s] for s in which], *[sources[s] for s in which]]).astype(jnp.int32)

    every = list(range(len(CHUNKS)))
    early, last = list(range(chips - 1)), [chips - 1]
    acc = add_product(
        info_of(early),
        [[[spread[h][c] for h in every] for c in slots[s]] for s in early],
        natural,
        residual_in,
        0,
        False,
    )
    for h in every:
        acc = add_product(
            info_of(last),
            [[[spread[h][c]] for c in slots[s]] for s in last],
            natural,
            acc,
            int(edges[h]) // TILE,
            True,
        )
    return acc


def solution(mesh):
    in_specs = (P("row", "col"), P("row", "col"), P(), P("row", "col"))
    out_specs = P("row", "col")
    body = functools.partial(on_device, mesh.shape["col"] // CORES, mesh.shape["row"])
    return jax.shard_map(body, mesh=mesh, in_specs=in_specs, out_specs=out_specs, check_vma=False)
```

```python
import functools

import jax
import jax.numpy as jnp
import numpy as np
from jax import lax
from jax.experimental import pallas as pl
from jax.experimental.pallas import tpu as pltpu
from jax.sharding import PartitionSpec as P

C_SLAB = 2
CORES = 2
TILE = 256
WHOLE_TILES = 4
CONTRACT_FIRST = (((0,), (0,)), ((), ()))


def round_up(value, step):
    return -(-value // step) * step


def stored_positions(irrep_virtual, chips, depth, depth_padded):
    pair_irrep = jnp.bitwise_xor(irrep_virtual[:C_SLAB][:, None], irrep_virtual[None, :]).reshape(-1)
    count = pair_irrep.shape[0]
    key = pair_irrep * count + jnp.arange(count, dtype=jnp.int32)
    blocks = jnp.pad(
        key.reshape(chips * CORES, depth), ((0, 0), (0, depth_padded - depth)), constant_values=-1
    ).reshape(chips, CORES * depth_padded, 1)
    rank = jnp.sum((key[None, None, :] < blocks).astype(jnp.int32), axis=2, keepdims=True)
    return jnp.where(blocks < 0, -1, rank)


def permute_kernel(count, has_previous, base_ref, pos_ref, *refs):
    out_ref = refs[-1]
    total = refs[count][0].astype(jnp.float32) if has_previous else None
    pos = pos_ref[0]
    for s in range(count):
        rows = refs[s].shape[0]
        picks = pos - base_ref[s] == lax.broadcasted_iota(jnp.int32, (pos.shape[0], rows), 1)
        term = jnp.dot(picks.astype(jnp.bfloat16), refs[s][...], preferred_element_type=jnp.float32)
        total = term if total is None else total + term
    out_ref[0] = total.astype(out_ref.dtype)


def add_permuted(pos, parts, bases, previous):
    chips, rows, _ = pos.shape
    columns = parts[0].shape[1]
    block = pl.BlockSpec((1, rows, columns), lambda q, *_: (q, 0, 0))
    in_specs = [pl.BlockSpec((1, rows, 1), lambda q, *_: (q, 0, 0))]
    in_specs += [
        pl.BlockSpec(part.shape, lambda q, *_: (0, 0), pipeline_mode=pl.Buffered(1)) for part in parts
    ]
    operands = [bases, pos, *parts]
    aliases = {}
    if previous is not None:
        in_specs.append(block)
        aliases = {len(operands): 0}
        operands.append(previous)
    return pl.pallas_call(
        functools.partial(permute_kernel, len(parts), previous is not None),
        grid_spec=pltpu.PrefetchScalarGridSpec(
            num_scalar_prefetch=1, grid=(chips,), in_specs=in_specs, out_specs=block
        ),
        out_shape=jax.ShapeDtypeStruct((chips, rows, columns), parts[0].dtype),
        input_output_aliases=aliases,
        compiler_params=pltpu.CompilerParams(vmem_limit_bytes=32 << 20),
        cost_estimate=pl.CostEstimate(
            flops=2 * chips * rows * columns * sum(part.shape[0] for part in parts),
            bytes_accessed=4 * chips * rows * columns,
            transcendentals=0,
        ),
    )(*operands)


def gather_integrals(values, size):
    half = round_up(values.shape[0] // 2, 16)

    def send(array, bit):
        return lax.ppermute(array, "row", [(i, i ^ bit) for i in range(size)])

    got = {0: [values]}
    order = sorted(range(1, size), key=lambda d: (bin(d).count("1"), d))
    for d in order:
        low, high = d & -d, 1 << (d.bit_length() - 1)
        if low == high:
            got[d] = [send(values, d)]
            continue
        parts = []
        for which, bit in ((0, low), (1, high)):
            source = got[d ^ bit]
            if len(source) == 2:
                piece = source[which]
            else:
                piece = source[0][:half] if which == 0 else source[0][half:]
            parts.append(send(piece, bit))
        got[d] = parts
    return got, order, half


def slot_table(chips):
    table = []
    for z in range(chips):
        line = []
        for s in range(1, chips):
            if z + s < chips:
                line.append((("L", s), z + s))
            if z - s >= 0:
                line.append((("R", s), z - s))
        table.append(line)
    return table


def spread_line(chunk, chips):
    got = {}
    swap_all = [(i, i ^ 1) for i in range(chips * CORES)]
    got["own", 0] = (chunk, lax.ppermute(chunk, "col", swap_all))
    held = {"L": chunk, "R": chunk}
    for s in range(1, chips):
        for way, step in (("L", -1), ("R", 1)):
            pairs = []
            ends = []
            for z in range(chips):
                source = z + s if step < 0 else z - s
                if 0 <= source < chips:
                    ends.append(z)
                    for core in range(CORES):
                        pairs.append(((z - step) * CORES + core, z * CORES + core))
            held[way] = lax.ppermute(held[way], "col", pairs)
            swap = [(z * CORES + core, z * CORES + 1 - core) for z in ends for core in range(CORES)]
            got[way, s] = (held[way], lax.ppermute(held[way], "col", swap))
    return got


def line_kernel(slots, first_slot, depth, info_ref, *refs):
    count = len(slots)
    offsets = np.cumsum([0, *slots])
    n_arrays = int(offsets[-1]) * CORES
    arrays = refs[:n_arrays]
    natural_ref, acc_ref = refs[n_arrays], refs[n_arrays + 1]
    out_ref, buffer, integrals, sems, sem_integrals = refs[n_arrays + 2 :]
    core = info_ref[0]
    tile = acc_ref.shape[0]
    i = pl.program_id(0)
    steps = arrays[0].shape[1] // tile

    def fetch(step, half):
        lanes = pl.ds(pl.multiple_of(step * tile, tile), tile)
        for s in range(count):
            for k in range(slots[s]):
                at = (int(offsets[s]) + k) * CORES

                def start(at=at, s=s):
                    for other in range(CORES):
                        place = jnp.where(core == other, 0, depth) + 2 * depth * s
                        pltpu.make_async_copy(
                            arrays[at + other].at[:, lanes],
                            buffer.at[half, pl.ds(pl.multiple_of(place, 16), depth), :],
                            sems.at[half],
                        ).start()

                if slots[s] == 1:
                    start()
                else:
                    pl.when(info_ref[1 + 2 * (first_slot + s)] == k)(start)

    @pl.when(i == 0)
    def _():
        for s in range(count):
            pltpu.make_async_copy(
                natural_ref.at[info_ref[2 + 2 * (first_slot + s)]],
                integrals.at[pl.ds(2 * depth * s, 2 * depth), :],
                sem_integrals,
            ).start()
        fetch(0, 0)

    @pl.when(i + 1 < steps)
    def _():
        fetch(i + 1, lax.rem(i + 1, 2))

    @pl.when(i == 0)
    def _():
        pltpu.make_async_copy(integrals, integrals, sem_integrals).wait()

    now = lax.rem(i, 2)
    pltpu.make_async_copy(buffer.at[now], buffer.at[now], sems.at[now]).wait()
    out_ref[...] = acc_ref[...] + lax.dot_general(
        buffer[now], integrals[...], CONTRACT_FIRST, preferred_element_type=jnp.float32
    )


def product_cost(lanes, rows, columns):
    return pl.CostEstimate(
        flops=2 * lanes * rows * columns,
        bytes_accessed=8 * lanes * columns + 2 * rows * (lanes + columns),
        transcendentals=0,
    )


def add_line(info, first_slot, slots, natural, acc, first_tile, in_place):
    tile = TILE
    depth, lanes = slots[0][0][0].shape
    columns = natural.shape[2]
    arrays = [a for slot in slots for pair in slot for a in pair]
    anywhere = pl.BlockSpec(memory_space=pl.ANY)
    block = pl.BlockSpec((tile, columns), lambda i, *_: (first_tile + i, 0))
    operands = [info, *arrays, natural, acc]
    rows = 2 * depth * len(slots)
    return pl.pallas_call(
        functools.partial(line_kernel, tuple(len(slot) for slot in slots), first_slot, depth),
        grid_spec=pltpu.PrefetchScalarGridSpec(
            num_scalar_prefetch=1,
            grid=(lanes // tile,),
            in_specs=[anywhere] * (len(arrays) + 1) + [block],
            out_specs=block,
            scratch_shapes=[
                pltpu.VMEM((2, rows, tile), natural.dtype),
                pltpu.VMEM((rows, columns), natural.dtype),
                pltpu.SemaphoreType.DMA((2,)),
                pltpu.SemaphoreType.DMA,
            ],
        ),
        out_shape=jax.ShapeDtypeStruct(acc.shape, acc.dtype),
        input_output_aliases={len(operands) - 1: 0} if in_place else {},
        compiler_params=pltpu.CompilerParams(vmem_limit_bytes=32 << 20),
        cost_estimate=product_cost(lanes, rows, columns),
    )(*operands)


def whole_kernel(t_ref, v_ref, residual_ref, acc_ref, out_ref):
    del acc_ref
    blocks, depth, tile = t_ref.shape
    out_ref[...] = residual_ref[...] + lax.dot_general(
        t_ref[...].reshape(blocks * depth, tile),
        v_ref[...].reshape(blocks * depth, -1),
        CONTRACT_FIRST,
        preferred_element_type=jnp.float32,
    )


def add_whole(gathered, natural, residual, acc):
    tile = TILE
    blocks, depth, lanes = gathered.shape
    columns = natural.shape[2]
    block = pl.BlockSpec((tile, columns), lambda i: (i, 0))
    return pl.pallas_call(
        whole_kernel,
        grid=(lanes // tile,),
        in_specs=[
            pl.BlockSpec((blocks, depth, tile), lambda i: (0, 0, i)),
            pl.BlockSpec(natural.shape, lambda i: (0, 0, 0), pipeline_mode=pl.Buffered(1)),
            block,
            pl.BlockSpec(memory_space=pl.ANY),
        ],
        out_specs=block,
        out_shape=jax.ShapeDtypeStruct(acc.shape, acc.dtype),
        input_output_aliases={3: 0},
        compiler_params=pltpu.CompilerParams(vmem_limit_bytes=32 << 20),
        cost_estimate=product_cost(lanes, blocks * depth, columns),
    )(gathered, natural, residual, acc)


def on_device(chips, row_size, amplitudes, values_stored, irrep_virtual, residual_in):
    occ, depth = amplitudes.shape
    depth_padded = round_up(depth, 16)
    stored_rows = values_stored.shape[0]
    edge = WHOLE_TILES * TILE
    lanes = round_up(occ, TILE)

    columns_first = jnp.pad(amplitudes.T, ((0, depth_padded - depth), (0, lanes - occ)))
    whole, chunk = columns_first[:, :edge], columns_first[:, edge:]
    gathered = lax.all_gather(whole, "col", axis=0)
    spread = spread_line(chunk, chips)
    got, order, half = gather_integrals(values_stored, row_size)

    pos = stored_positions(irrep_virtual, chips, depth, depth_padded)
    groups = [[(0, 0)], [(d, 0) for d in order if len(got[d]) == 1]]
    groups += [[(d, 0), (d, 1)] for d in order if len(got[d]) == 2]
    natural = None
    starts = [
        [[(r ^ d) * stored_rows + which * half for d, which in group] for group in groups]
        for r in range(row_size)
    ]
    width = max(len(group) for group in groups)
    starts = np.array([[g + [0] * (width - len(g)) for g in of_row] for of_row in starts], np.int32)
    bases = jnp.asarray(starts)[lax.axis_index("row")]
    for g, group in enumerate(groups):
        natural = add_permuted(pos, [got[d][which] for d, which in group], bases[g], natural)

    table = slot_table(chips)
    slots = [[("own", 0)]]
    slots += [sorted({table[z][t][0] for z in range(chips)}) for t in range(chips - 1)]
    rows_of_info = []
    for device in range(chips * CORES):
        z = device // CORES
        line = [device % CORES, 0, z]
        for t in range(chips - 1):
            line += [slots[t + 1].index(table[z][t][0]), table[z][t][1]]
        rows_of_info.append(line)
    info = jnp.asarray(np.array(rows_of_info, np.int32))[lax.axis_index("col")]

    arrays = [[spread[c] for c in slot] for slot in slots]
    last = chips - 1
    acc = add_line(info, 0, arrays[:last], natural, residual_in, WHOLE_TILES, False)
    acc = add_whole(gathered, natural, residual_in, acc)
    return add_line(info, last, arrays[last:], natural, acc, WHOLE_TILES, True)


def solution(mesh):
    in_specs = (P("row", "col"), P("row", "col"), P(), P("row", "col"))
    out_specs = P("row", "col")
    body = functools.partial(on_device, mesh.shape["col"] // CORES, mesh.shape["row"])
    return jax.shard_map(body, mesh=mesh, in_specs=in_specs, out_specs=out_specs, check_vma=False)
```

```python
import functools

import jax
import jax.numpy as jnp
import numpy as np
from jax import lax
from jax.experimental import pallas as pl
from jax.experimental.pallas import tpu as pltpu
from jax.sharding import PartitionSpec as P

C_SLAB = 2
CORES = 2
TILE = 256
VMEM_BYTES = 58 << 20
WHOLE_TILES = 4
CONTRACT_FIRST = (((0,), (0,)), ((), ()))


def round_up(value, step):
    return -(-value // step) * step


def stored_positions(irrep_virtual, chips, depth, depth_padded):
    pair_irrep = jnp.bitwise_xor(irrep_virtual[:C_SLAB][:, None], irrep_virtual[None, :]).reshape(-1)
    count = pair_irrep.shape[0]
    key = pair_irrep * count + jnp.arange(count, dtype=jnp.int32)
    blocks = jnp.pad(
        key.reshape(chips * CORES, depth), ((0, 0), (0, depth_padded - depth)), constant_values=-1
    ).reshape(chips, CORES * depth_padded, 1)
    rank = jnp.sum((key[None, None, :] < blocks).astype(jnp.int32), axis=2, keepdims=True)
    return jnp.where(blocks < 0, -1, rank)


def permute_kernel(count, has_previous, base_ref, pos_ref, *refs):
    out_ref = refs[-1]
    total = refs[count][0].astype(jnp.float32) if has_previous else None
    pos = pos_ref[0]
    for s in range(count):
        rows = refs[s].shape[0]
        picks = pos - base_ref[s] == lax.broadcasted_iota(jnp.int32, (pos.shape[0], rows), 1)
        term = jnp.dot(picks.astype(jnp.bfloat16), refs[s][...], preferred_element_type=jnp.float32)
        total = term if total is None else total + term
    out_ref[0] = total.astype(out_ref.dtype)


def add_permuted(pos, parts, bases, previous):
    chips, rows, _ = pos.shape
    columns = parts[0].shape[1]
    block = pl.BlockSpec((1, rows, columns), lambda q, *_: (q, 0, 0))
    in_specs = [pl.BlockSpec((1, rows, 1), lambda q, *_: (q, 0, 0))]
    in_specs += [
        pl.BlockSpec(part.shape, lambda q, *_: (0, 0), pipeline_mode=pl.Buffered(1)) for part in parts
    ]
    operands = [bases, pos, *parts]
    aliases = {}
    if previous is not None:
        in_specs.append(block)
        aliases = {len(operands): 0}
        operands.append(previous)
    return pl.pallas_call(
        functools.partial(permute_kernel, len(parts), previous is not None),
        grid_spec=pltpu.PrefetchScalarGridSpec(
            num_scalar_prefetch=1, grid=(chips,), in_specs=in_specs, out_specs=block
        ),
        out_shape=jax.ShapeDtypeStruct((chips, rows, columns), parts[0].dtype),
        input_output_aliases=aliases,
        compiler_params=pltpu.CompilerParams(vmem_limit_bytes=VMEM_BYTES),
        cost_estimate=pl.CostEstimate(
            flops=2 * chips * rows * columns * sum(part.shape[0] for part in parts),
            bytes_accessed=4 * chips * rows * columns,
            transcendentals=0,
        ),
    )(*operands)


def gather_integrals(values, size):
    half = round_up(values.shape[0] // 2, 16)

    def send(array, bit):
        return lax.ppermute(array, "row", [(i, i ^ bit) for i in range(size)])

    got = {0: [values]}
    order = sorted(range(1, size), key=lambda d: (bin(d).count("1"), d))
    for d in order:
        low, high = d & -d, 1 << (d.bit_length() - 1)
        if low == high:
            got[d] = [send(values, d)]
            continue
        parts = []
        for which, bit in ((0, low), (1, high)):
            source = got[d ^ bit]
            if len(source) == 2:
                piece = source[which]
            else:
                piece = source[0][:half] if which == 0 else source[0][half:]
            parts.append(send(piece, bit))
        got[d] = parts
    return got, order, half


def slot_table(chips):
    table = []
    for z in range(chips):
        line = []
        for s in range(1, chips):
            if z + s < chips:
                line.append((("L", s), z + s))
            if z - s >= 0:
                line.append((("R", s), z - s))
        table.append(line)
    return table


def line_step(held, s, chips):
    arrived = {}
    for way, step in (("L", -1), ("R", 1)):
        pairs = []
        for z in range(chips):
            if 0 <= z - step * s < chips:
                pairs += [((z - step) * CORES + core, z * CORES + core) for core in range(CORES)]
        arrived[way] = lax.ppermute(held[way], "col", pairs)
    return arrived


def swap_cores(block, way, s, chips):
    step = {"L": -1, "R": 1}[way]
    pairs = []
    for z in range(chips):
        if 0 <= z - step * s < chips:
            pairs += [(z * CORES + core, z * CORES + 1 - core) for core in range(CORES)]
    return lax.ppermute(block, "col", pairs)


def line_kernel(slots, first_slot, depth, info_ref, *refs):
    count = len(slots)
    offsets = np.cumsum([0, *slots])
    n_arrays = int(offsets[-1]) * CORES
    arrays = refs[:n_arrays]
    natural_ref, acc_ref = refs[n_arrays], refs[n_arrays + 1]
    out_ref, buffer, integrals, sems, sem_integrals = refs[n_arrays + 2 :]
    core = info_ref[0]
    tile = acc_ref.shape[0]
    i = pl.program_id(0)
    steps = arrays[0].shape[1] // tile

    def fetch(step, half):
        lanes = pl.ds(pl.multiple_of(step * tile, tile), tile)
        for s in range(count):
            for k in range(slots[s]):
                at = (int(offsets[s]) + k) * CORES

                def start(at=at, s=s):
                    for other in range(CORES):
                        place = jnp.where(core == other, 0, depth) + 2 * depth * s
                        pltpu.make_async_copy(
                            arrays[at + other].at[:, lanes],
                            buffer.at[half, pl.ds(pl.multiple_of(place, 16), depth), :],
                            sems.at[half],
                        ).start()

                if slots[s] == 1:
                    start()
                else:
                    pl.when(info_ref[1 + 2 * (first_slot + s)] == k)(start)

    @pl.when(i == 0)
    def _():
        for s in range(count):
            pltpu.make_async_copy(
                natural_ref.at[info_ref[2 + 2 * (first_slot + s)]],
                integrals.at[pl.ds(2 * depth * s, 2 * depth), :],
                sem_integrals,
            ).start()
        fetch(0, 0)

    @pl.when(i + 1 < steps)
    def _():
        fetch(i + 1, lax.rem(i + 1, 2))

    @pl.when(i == 0)
    def _():
        pltpu.make_async_copy(integrals, integrals, sem_integrals).wait()

    now = lax.rem(i, 2)
    pltpu.make_async_copy(buffer.at[now], buffer.at[now], sems.at[now]).wait()
    out_ref[...] = acc_ref[...] + lax.dot_general(
        buffer[now], integrals[...], CONTRACT_FIRST, preferred_element_type=jnp.float32
    )


def product_cost(lanes, rows, columns):
    return pl.CostEstimate(
        flops=2 * lanes * rows * columns,
        bytes_accessed=8 * lanes * columns + 2 * rows * (lanes + columns),
        transcendentals=0,
    )


def add_line(info, first_slot, slots, natural, acc, first_tile, in_place):
    tile = TILE
    depth, lanes = slots[0][0][0].shape
    columns = natural.shape[2]
    arrays = [a for slot in slots for pair in slot for a in pair]
    anywhere = pl.BlockSpec(memory_space=pl.ANY)
    block = pl.BlockSpec((tile, columns), lambda i, *_: (first_tile + i, 0))
    operands = [info, *arrays, natural, acc]
    rows = 2 * depth * len(slots)
    return pl.pallas_call(
        functools.partial(line_kernel, tuple(len(slot) for slot in slots), first_slot, depth),
        grid_spec=pltpu.PrefetchScalarGridSpec(
            num_scalar_prefetch=1,
            grid=(lanes // tile,),
            in_specs=[anywhere] * (len(arrays) + 1) + [block],
            out_specs=block,
            scratch_shapes=[
                pltpu.VMEM((2, rows, tile), natural.dtype),
                pltpu.VMEM((rows, columns), natural.dtype),
                pltpu.SemaphoreType.DMA((2,)),
                pltpu.SemaphoreType.DMA,
            ],
        ),
        out_shape=jax.ShapeDtypeStruct(acc.shape, acc.dtype),
        input_output_aliases={len(operands) - 1: 0} if in_place else {},
        compiler_params=pltpu.CompilerParams(vmem_limit_bytes=VMEM_BYTES),
        cost_estimate=product_cost(lanes, rows, columns),
    )(*operands)


def whole_kernel(t_ref, v_ref, residual_ref, acc_ref, out_ref):
    del acc_ref
    blocks, depth, tile = t_ref.shape
    out_ref[...] = residual_ref[...] + lax.dot_general(
        t_ref[...].reshape(blocks * depth, tile),
        v_ref[...].reshape(blocks * depth, -1),
        CONTRACT_FIRST,
        preferred_element_type=jnp.float32,
    )


def add_whole(gathered, natural, residual, acc):
    tile = TILE
    blocks, depth, lanes = gathered.shape
    columns = natural.shape[2]
    block = pl.BlockSpec((tile, columns), lambda i: (i, 0))
    return pl.pallas_call(
        whole_kernel,
        grid=(lanes // tile,),
        in_specs=[
            pl.BlockSpec((blocks, depth, tile), lambda i: (0, 0, i)),
            pl.BlockSpec(natural.shape, lambda i: (0, 0, 0), pipeline_mode=pl.Buffered(1)),
            block,
            pl.BlockSpec(memory_space=pl.ANY),
        ],
        out_specs=block,
        out_shape=jax.ShapeDtypeStruct(acc.shape, acc.dtype),
        input_output_aliases={3: 0},
        compiler_params=pltpu.CompilerParams(vmem_limit_bytes=VMEM_BYTES),
        cost_estimate=product_cost(lanes, blocks * depth, columns),
    )(gathered, natural, residual, acc)


def on_device(chips, row_size, amplitudes, values_stored, irrep_virtual, residual_in):
    occ, depth = amplitudes.shape
    depth_padded = round_up(depth, 16)
    stored_rows = values_stored.shape[0]
    edge = WHOLE_TILES * TILE
    lanes = round_up(occ, TILE)

    columns_first = jnp.pad(amplitudes.T, ((0, depth_padded - depth), (0, lanes - occ)))
    whole, chunk = columns_first[:, :edge], columns_first[:, edge:]
    gathered = lax.all_gather(whole, "col", axis=0)
    held = line_step({"L": chunk, "R": chunk}, 1, chips)
    got, order, half = gather_integrals(values_stored, row_size)
    spread = {("own", 0): (chunk, swap_cores(chunk, "L", 0, chips))}

    pos = stored_positions(irrep_virtual, chips, depth, depth_padded)
    groups = [[(0, 0)], [(d, 0) for d in order if len(got[d]) == 1]]
    groups += [[(d, 0), (d, 1)] for d in order if len(got[d]) == 2]
    starts = [
        [[(r ^ d) * stored_rows + which * half for d, which in group] for group in groups]
        for r in range(row_size)
    ]
    width = max(len(group) for group in groups)
    starts = np.array([[g + [0] * (width - len(g)) for g in of_row] for of_row in starts], np.int32)
    bases = jnp.asarray(starts)[lax.axis_index("row")]
    naturals = [None]
    for g, group in enumerate(groups):
        naturals.append(add_permuted(pos, [got[d][which] for d, which in group], bases[g], naturals[-1]))
        s = g + 1
        if s < chips - 1:
            held["L"], held["R"], naturals[-1] = lax.optimization_barrier((held["L"], held["R"], naturals[-1]))
            following = line_step(held, s + 1, chips)
            for way in ("L", "R"):
                spread[way, s] = (held[way], swap_cores(held[way], way, s, chips))
            held = following
    for s in range(len(groups) + 1, chips - 1):
        following = line_step(held, s + 1, chips)
        for way in ("L", "R"):
            spread[way, s] = (held[way], swap_cores(held[way], way, s, chips))
        held = following
    natural = naturals[-1]

    table = slot_table(chips)
    slots = [[("own", 0)]]
    slots += [sorted({table[z][t][0] for z in range(chips)}) for t in range(chips - 1)]
    rows_of_info = []
    for device in range(chips * CORES):
        z = device // CORES
        line = [device % CORES, 0, z]
        for t in range(chips - 1):
            line += [slots[t + 1].index(table[z][t][0]), table[z][t][1]]
        rows_of_info.append(line)
    info = jnp.asarray(np.array(rows_of_info, np.int32))[lax.axis_index("col")]

    last = chips - 1
    early = [[spread[c] for c in slot] for slot in slots[:last]]
    acc = add_line(info, 0, early, natural, residual_in, WHOLE_TILES, False)
    held["L"], held["R"], acc = lax.optimization_barrier((held["L"], held["R"], acc))
    for way in ("L", "R"):
        spread[way, last] = (held[way], swap_cores(held[way], way, last, chips))
    acc = add_whole(gathered, natural, residual_in, acc)
    return add_line(info, last, [[spread[c] for c in slots[last]]], natural, acc, WHOLE_TILES, True)


def solution(mesh):
    in_specs = (P("row", "col"), P("row", "col"), P(), P("row", "col"))
    out_specs = P("row", "col")
    body = functools.partial(on_device, mesh.shape["col"] // CORES, mesh.shape["row"])
    return jax.shard_map(body, mesh=mesh, in_specs=in_specs, out_specs=out_specs, check_vma=False)
```

```python
import functools

import jax
import jax.numpy as jnp
import numpy as np
from jax import lax
from jax.experimental import pallas as pl
from jax.experimental.pallas import tpu as pltpu
from jax.sharding import PartitionSpec as P

C_SLAB = 2
CORES = 2
LANES = 128
SUBLANES = 8
TILE = 256
VMEM_BYTES = 58 << 20
WHOLE_TILES = 4
CONTRACT_FIRST = (((0,), (0,)), ((), ()))


def round_up(value, step):
    return -(-value // step) * step


def stored_positions(irrep_virtual, chips, depth, depth_padded):
    pair_irrep = jnp.bitwise_xor(irrep_virtual[:C_SLAB][:, None], irrep_virtual[None, :]).reshape(-1)
    count = pair_irrep.shape[0]
    key = pair_irrep * count + jnp.arange(count, dtype=jnp.int32)
    rank = jnp.sum((key[:, None] < key[None, :]).astype(jnp.int32), axis=0)
    return jnp.pad(rank.reshape(chips * CORES, depth), ((0, 0), (0, depth_padded - depth))).reshape(-1)


def gather_kernel(firsts, depth_of, place_ref, *refs):
    parts, (out_ref, rows_ref, taken_ref) = refs[: len(firsts)], refs[len(firsts) :]
    total, columns = out_ref.shape
    tiles = -(-columns // LANES)
    per_eight = depth_of * SUBLANES
    widths = [min(LANES, columns - t * LANES) for t in range(tiles)]
    i = pl.program_id(0)

    @pl.when(i == 0)
    def _():
        for part, first in zip(parts, firsts):
            height = part.shape[0]

            def spread_rows(values, at):
                for top in range(0, values.shape[0], SUBLANES):
                    eight = values[top : top + SUBLANES].astype(jnp.float32)
                    for t, width in enumerate(widths):
                        base = at + top // SUBLANES * per_eight + t * SUBLANES
                        rows_ref[pl.ds(base, eight.shape[0]), 0:width] = eight[:, t * LANES : t * LANES + width]

            def body(g, carry, part=part, first=first, spread_rows=spread_rows):
                at = pl.multiple_of((first // SUBLANES + 2 * g) * per_eight, per_eight)
                spread_rows(part[pl.ds(pl.multiple_of(g * 16, 16), 16), :], at)
                return carry

            whole = height // 16
            lax.fori_loop(0, whole, body, 0)
            if height > whole * 16:
                spread_rows(part[whole * 16 : height, :], (first // SUBLANES + 2 * whole) * per_eight)

    def take(g, carry):
        for u in range(16):
            place = place_ref[i * total + g * 16 + u]
            target = g * 2 * per_eight + u // SUBLANES * per_eight + u % SUBLANES
            taken_ref[pl.ds(target, depth_of, stride=SUBLANES), :] = rows_ref[
                pl.ds(place, depth_of, stride=SUBLANES), :
            ]
        return carry

    lax.fori_loop(0, total // 16, take, 0)

    def put(g, carry):
        for t, width in enumerate(widths):
            pieces = [
                taken_ref[pl.ds(pl.multiple_of((2 * g + e) * per_eight + t * SUBLANES, SUBLANES), SUBLANES), 0:width]
                for e in range(2)
            ]
            out_ref[pl.ds(pl.multiple_of(g * 16, 16), 16), t * LANES : t * LANES + width] = jnp.concatenate(
                pieces, axis=0
            ).astype(out_ref.dtype)
        return carry

    lax.fori_loop(0, total // 16, put, 0)


def natural_rows(rank, parts, row, stored_rows, chips):
    columns = parts[0][0].shape[1]
    block_rows = round_up(stored_rows, 16)
    blocks = 1 + max(distance for _, distance, _ in parts)
    depth_of = round_up(-(-columns // LANES), SUBLANES)
    at = ((rank // stored_rows) ^ row) * block_rows + rank % stored_rows
    place = at // SUBLANES * (depth_of * SUBLANES) + at % SUBLANES
    step_rows = rank.shape[0] // chips
    firsts = tuple(distance * block_rows + first for _, distance, first in parts)
    natural = pl.pallas_call(
        functools.partial(gather_kernel, firsts, depth_of),
        grid_spec=pltpu.PrefetchScalarGridSpec(
            num_scalar_prefetch=1,
            grid=(chips,),
            in_specs=[
                pl.BlockSpec(part.shape, lambda q, *_: (0, 0), pipeline_mode=pl.Buffered(1)) for part, _, _ in parts
            ],
            out_specs=pl.BlockSpec((step_rows, columns), lambda q, *_: (q, 0)),
            scratch_shapes=[
                pltpu.VMEM((blocks * block_rows * depth_of, LANES), jnp.float32),
                pltpu.VMEM((step_rows * depth_of, LANES), jnp.float32),
            ],
        ),
        out_shape=jax.ShapeDtypeStruct((rank.shape[0], columns), parts[0][0].dtype),
        compiler_params=pltpu.CompilerParams(vmem_limit_bytes=VMEM_BYTES),
        cost_estimate=pl.CostEstimate(flops=15 * 10**9, bytes_accessed=4 * rank.shape[0] * columns, transcendentals=0),
    )(place, *[part for part, _, _ in parts])
    return natural.reshape(chips, step_rows, columns)


def gather_integrals(values, size):
    half = round_up(values.shape[0] // 2, 16)

    def send(array, bit):
        return lax.ppermute(array, "row", [(i, i ^ bit) for i in range(size)])

    got = {0: [values]}
    order = sorted(range(1, size), key=lambda d: (bin(d).count("1"), d))
    for d in order:
        low, high = d & -d, 1 << (d.bit_length() - 1)
        if low == high:
            got[d] = [send(values, d)]
            continue
        parts = []
        for which, bit in ((0, low), (1, high)):
            source = got[d ^ bit]
            if len(source) == 2:
                piece = source[which]
            else:
                piece = source[0][:half] if which == 0 else source[0][half:]
            parts.append(send(piece, bit))
        got[d] = parts
    return got, order, half


def slot_table(chips):
    table = []
    for z in range(chips):
        line = []
        for s in range(1, chips):
            if z + s < chips:
                line.append((("L", s), z + s))
            if z - s >= 0:
                line.append((("R", s), z - s))
        table.append(line)
    return table


def line_step(held, s, chips):
    arrived = {}
    for way, step in (("L", -1), ("R", 1)):
        pairs = []
        for z in range(chips):
            if 0 <= z - step * s < chips:
                pairs += [((z - step) * CORES + core, z * CORES + core) for core in range(CORES)]
        arrived[way] = lax.ppermute(held[way], "col", pairs)
    return arrived


def swap_cores(block, way, s, chips):
    step = {"L": -1, "R": 1}[way]
    pairs = []
    for z in range(chips):
        if 0 <= z - step * s < chips:
            pairs += [(z * CORES + core, z * CORES + 1 - core) for core in range(CORES)]
    return lax.ppermute(block, "col", pairs)


def line_kernel(slots, first_slot, depth, info_ref, *refs):
    count = len(slots)
    offsets = np.cumsum([0, *slots])
    n_arrays = int(offsets[-1]) * CORES
    arrays = refs[:n_arrays]
    natural_ref, residual_ref, _ = refs[n_arrays : n_arrays + 3]
    out_ref, buffer, integrals, sems, sem_integrals = refs[n_arrays + 3 :]
    core = info_ref[0]
    tile = residual_ref.shape[0]
    i = pl.program_id(0)
    steps = arrays[0].shape[1] // tile

    def fetch(step, half):
        lanes = pl.ds(pl.multiple_of(step * tile, tile), tile)
        for s in range(count):
            for k in range(slots[s]):
                at = (int(offsets[s]) + k) * CORES

                def start(at=at, s=s):
                    for other in range(CORES):
                        place = jnp.where(core == other, 0, depth) + 2 * depth * s
                        pltpu.make_async_copy(
                            arrays[at + other].at[:, lanes],
                            buffer.at[half, pl.ds(pl.multiple_of(place, 16), depth), :],
                            sems.at[half],
                        ).start()

                if slots[s] == 1:
                    start()
                else:
                    pl.when(info_ref[1 + 2 * (first_slot + s)] == k)(start)

    @pl.when(i == 0)
    def _():
        for s in range(count):
            pltpu.make_async_copy(
                natural_ref.at[info_ref[2 + 2 * (first_slot + s)]],
                integrals.at[pl.ds(2 * depth * s, 2 * depth), :],
                sem_integrals,
            ).start()
        fetch(0, 0)

    @pl.when(i + 1 < steps)
    def _():
        fetch(i + 1, lax.rem(i + 1, 2))

    @pl.when(i == 0)
    def _():
        pltpu.make_async_copy(integrals, integrals, sem_integrals).wait()

    now = lax.rem(i, 2)
    pltpu.make_async_copy(buffer.at[now], buffer.at[now], sems.at[now]).wait()
    out_ref[...] = residual_ref[...] + lax.dot_general(
        buffer[now], integrals[...], CONTRACT_FIRST, preferred_element_type=jnp.float32
    )


def product_cost(lanes, rows, columns):
    return pl.CostEstimate(
        flops=2 * lanes * rows * columns,
        bytes_accessed=8 * lanes * columns + 2 * rows * (lanes + columns),
        transcendentals=0,
    )


def add_line(info, first_slot, slots, natural, residual, acc, first_tile):
    tile = TILE
    depth, lanes = slots[0][0][0].shape
    columns = natural.shape[2]
    arrays = [a for slot in slots for pair in slot for a in pair]
    anywhere = pl.BlockSpec(memory_space=pl.ANY)
    block = pl.BlockSpec((tile, columns), lambda i, *_: (first_tile + i, 0))
    operands = [info, *arrays, natural, residual, acc]
    rows = 2 * depth * len(slots)
    return pl.pallas_call(
        functools.partial(line_kernel, tuple(len(slot) for slot in slots), first_slot, depth),
        grid_spec=pltpu.PrefetchScalarGridSpec(
            num_scalar_prefetch=1,
            grid=(lanes // tile,),
            in_specs=[anywhere] * (len(arrays) + 1) + [block, anywhere],
            out_specs=block,
            scratch_shapes=[
                pltpu.VMEM((2, rows, tile), natural.dtype),
                pltpu.VMEM((rows, columns), natural.dtype),
                pltpu.SemaphoreType.DMA((2,)),
                pltpu.SemaphoreType.DMA,
            ],
        ),
        out_shape=jax.ShapeDtypeStruct(acc.shape, acc.dtype),
        input_output_aliases={len(operands) - 1: 0},
        compiler_params=pltpu.CompilerParams(vmem_limit_bytes=VMEM_BYTES),
        cost_estimate=product_cost(lanes, rows, columns),
    )(*operands)


def whole_kernel(t_ref, v_ref, residual_ref, out_ref):
    blocks, depth, tile = t_ref.shape
    out_ref[...] = residual_ref[...] + lax.dot_general(
        t_ref[...].reshape(blocks * depth, tile),
        v_ref[...].reshape(blocks * depth, -1),
        CONTRACT_FIRST,
        preferred_element_type=jnp.float32,
    )


def add_whole(gathered, natural, residual):
    tile = TILE
    blocks, depth, lanes = gathered.shape
    columns = natural.shape[2]
    block = pl.BlockSpec((tile, columns), lambda i: (i, 0))
    return pl.pallas_call(
        whole_kernel,
        grid=(lanes // tile,),
        in_specs=[
            pl.BlockSpec((blocks, depth, tile), lambda i: (0, 0, i)),
            pl.BlockSpec(natural.shape, lambda i: (0, 0, 0), pipeline_mode=pl.Buffered(1)),
            block,
        ],
        out_specs=block,
        out_shape=jax.ShapeDtypeStruct(residual.shape, residual.dtype),
        compiler_params=pltpu.CompilerParams(vmem_limit_bytes=VMEM_BYTES),
        cost_estimate=product_cost(lanes, blocks * depth, columns),
    )(gathered, natural, residual)


def on_device(chips, row_size, amplitudes, values_stored, irrep_virtual, residual_in):
    occ, depth = amplitudes.shape
    depth_padded = round_up(depth, 16)
    stored_rows = values_stored.shape[0]
    edge = WHOLE_TILES * TILE
    lanes = round_up(occ, TILE)

    columns_first = jnp.pad(amplitudes.T, ((0, depth_padded - depth), (0, lanes - occ)))
    whole, chunk = columns_first[:, :edge], columns_first[:, edge:]
    gathered = lax.all_gather(whole, "col", axis=0)
    held = line_step({"L": chunk, "R": chunk}, 1, chips)
    got, order, half = gather_integrals(values_stored, row_size)
    parts = [(piece, d, half * which) for d in got for which, piece in enumerate(got[d])]
    rank = stored_positions(irrep_virtual, chips, depth, depth_padded)

    travelled = [("own", 0, chunk)]
    for s in range(1, chips - 1):
        travelled += [(way, s, held[way]) for way in ("L", "R")]
        held = line_step(held, s + 1, chips)
    blocks = lax.optimization_barrier(tuple(block for _, _, block in travelled))
    spread = {}
    for (way, s, _), block in zip(travelled, blocks):
        spread[way, s] = (block, swap_cores(block, "L" if way == "own" else way, s, chips))
    natural = natural_rows(rank, parts, lax.axis_index("row"), stored_rows, chips)

    table = slot_table(chips)
    slots = [[("own", 0)]]
    slots += [sorted({table[z][t][0] for z in range(chips)}) for t in range(chips - 1)]
    rows_of_info = []
    for device in range(chips * CORES):
        z = device // CORES
        line = [device % CORES, 0, z]
        for t in range(chips - 1):
            line += [slots[t + 1].index(table[z][t][0]), table[z][t][1]]
        rows_of_info.append(line)
    info = jnp.asarray(np.array(rows_of_info, np.int32))[lax.axis_index("col")]

    last = chips - 1
    held["L"], held["R"], natural = lax.optimization_barrier((held["L"], held["R"], natural))
    for way in ("L", "R"):
        spread[way, last] = (held[way], swap_cores(held[way], way, last, chips))
    acc = add_whole(gathered, natural, residual_in)
    return add_line(info, 0, [[spread[c] for c in slot] for slot in slots], natural, residual_in, acc, WHOLE_TILES)


def solution(mesh):
    in_specs = (P("row", "col"), P("row", "col"), P(), P("row", "col"))
    out_specs = P("row", "col")
    body = functools.partial(on_device, mesh.shape["col"] // CORES, mesh.shape["row"])
    return jax.shard_map(body, mesh=mesh, in_specs=in_specs, out_specs=out_specs, check_vma=False)
```

```python
import functools

import jax
import jax.numpy as jnp
import numpy as np
from jax import lax
from jax.experimental import pallas as pl
from jax.experimental.pallas import tpu as pltpu
from jax.sharding import PartitionSpec as P

C_SLAB = 2
CORES = 2
TILE = 256
VMEM_BYTES = 58 << 20
WHOLE_TILES = (4, 2)
CONTRACT_FIRST = (((0,), (0,)), ((), ()))


def round_up(value, step):
    return -(-value // step) * step


def stored_positions(irrep_virtual, chips, depth, depth_padded):
    pair_irrep = jnp.bitwise_xor(irrep_virtual[:C_SLAB][:, None], irrep_virtual[None, :]).reshape(-1)
    count = pair_irrep.shape[0]
    key = pair_irrep * count + jnp.arange(count, dtype=jnp.int32)
    blocks = jnp.pad(
        key.reshape(chips * CORES, depth), ((0, 0), (0, depth_padded - depth)), constant_values=-1
    ).reshape(chips, CORES * depth_padded, 1)
    rank = jnp.sum((key[None, None, :] < blocks).astype(jnp.int32), axis=2, keepdims=True)
    return jnp.where(blocks < 0, -1, rank)


def permute_kernel(groups, has_previous, base_ref, pos_ref, *refs):
    count = sum(len(group) for group in groups)
    out_ref = refs[count + has_previous]
    joined = list(refs[count + has_previous + 1 :])
    total = refs[count][0].astype(jnp.float32) if has_previous else None
    pos = pos_ref[0]
    for group in groups:
        if len(group) == 1:
            rows_ref = refs[group[0]]
        else:
            rows_ref = joined.pop(0)

            @pl.when(pl.program_id(0) == 0)
            def _(group=group, rows_ref=rows_ref):
                at = 0
                for p in group:
                    rows_ref[at : at + refs[p].shape[0], :] = refs[p][...]
                    at += refs[p].shape[0]

        rows = rows_ref.shape[0]
        picks = pos - base_ref[group[0]] == lax.broadcasted_iota(jnp.int32, (pos.shape[0], rows), 1)
        term = jnp.dot(picks.astype(jnp.bfloat16), rows_ref[...], preferred_element_type=jnp.float32)
        total = term if total is None else total + term
    out_ref[0] = total.astype(out_ref.dtype)


def add_permuted(pos, blocks, bases, previous):
    chips, rows, _ = pos.shape
    parts = [part for block in blocks for part in block]
    columns = parts[0].shape[1]
    numbers = iter(range(len(parts)))
    groups = tuple(tuple(next(numbers) for _ in block) for block in blocks)
    joined = [
        pltpu.VMEM((sum(part.shape[0] for part in block), columns), parts[0].dtype) for block in blocks if len(block) > 1
    ]
    block_spec = pl.BlockSpec((1, rows, columns), lambda q, *_: (q, 0, 0))
    in_specs = [pl.BlockSpec((1, rows, 1), lambda q, *_: (q, 0, 0))]
    in_specs += [pl.BlockSpec(part.shape, lambda q, *_: (0, 0), pipeline_mode=pl.Buffered(1)) for part in parts]
    operands = [bases, pos, *parts]
    aliases = {}
    if previous is not None:
        in_specs.append(block_spec)
        aliases = {len(operands): 0}
        operands.append(previous)
    return pl.pallas_call(
        functools.partial(permute_kernel, groups, previous is not None),
        grid_spec=pltpu.PrefetchScalarGridSpec(
            num_scalar_prefetch=1, grid=(chips,), in_specs=in_specs, out_specs=block_spec, scratch_shapes=joined
        ),
        out_shape=jax.ShapeDtypeStruct((chips, rows, columns), parts[0].dtype),
        input_output_aliases=aliases,
        compiler_params=pltpu.CompilerParams(vmem_limit_bytes=VMEM_BYTES),
        cost_estimate=pl.CostEstimate(
            flops=2 * chips * rows * columns * sum(part.shape[0] for part in parts),
            bytes_accessed=4 * chips * rows * columns,
            transcendentals=0,
        ),
    )(*operands)


def gather_integrals(values, size):
    half = round_up(values.shape[0] // 2, 16)

    def send(array, bit):
        return lax.ppermute(array, "row", [(i, i ^ bit) for i in range(size)])

    got = {0: [values]}
    order = sorted(range(1, size), key=lambda d: (bin(d).count("1"), d))
    for d in order:
        low, high = d & -d, 1 << (d.bit_length() - 1)
        if low == high:
            got[d] = [send(values, d)]
            continue
        parts = []
        for which, bit in ((0, low), (1, high)):
            source = got[d ^ bit]
            if len(source) == 2:
                piece = source[which]
            else:
                piece = source[0][:half] if which == 0 else source[0][half:]
            parts.append(send(piece, bit))
        got[d] = parts
    return got, order, half


def send_chips(block, distance, chips):
    pairs = [(z * CORES + core, (z ^ distance) * CORES + core) for z in range(chips) for core in range(CORES)]
    return lax.ppermute(block, "col", pairs)


def swap_cores(block, chips):
    return lax.ppermute(block, "col", [(i, i ^ 1) for i in range(chips * CORES)])


def direct_kernel(depth, info_ref, *refs):
    natural_ref, residual_ref, out_ref, buffer, integrals, sems, sem_integrals = refs[-7:]
    arrays = refs[:-7]
    count = len(arrays) // CORES
    core = info_ref[0]
    tile = residual_ref.shape[0]
    i = pl.program_id(0)
    steps = arrays[0].shape[1] // tile

    def fetch(step, half):
        lanes = pl.ds(pl.multiple_of(step * tile, tile), tile)
        for s in range(count):
            for other in range(CORES):
                place = jnp.where(core == other, 0, depth) + CORES * depth * s
                pltpu.make_async_copy(
                    arrays[CORES * s + other].at[:, lanes],
                    buffer.at[half, pl.ds(pl.multiple_of(place, 16), depth), :],
                    sems.at[half],
                ).start()

    @pl.when(i == 0)
    def _():
        for s in range(count):
            pltpu.make_async_copy(
                natural_ref.at[info_ref[1 + s]],
                integrals.at[pl.ds(CORES * depth * s, CORES * depth), :],
                sem_integrals,
            ).start()
        fetch(0, 0)

    @pl.when(i + 1 < steps)
    def _():
        fetch(i + 1, lax.rem(i + 1, 2))

    @pl.when(i == 0)
    def _():
        pltpu.make_async_copy(integrals, integrals, sem_integrals).wait()

    now = lax.rem(i, 2)
    pltpu.make_async_copy(buffer.at[now], buffer.at[now], sems.at[now]).wait()
    out_ref[...] = residual_ref[...] + lax.dot_general(
        buffer[now], integrals[...], CONTRACT_FIRST, preferred_element_type=jnp.float32
    )


def product_cost(lanes, rows, columns):
    return pl.CostEstimate(
        flops=2 * lanes * rows * columns,
        bytes_accessed=8 * lanes * columns + 2 * rows * (lanes + columns),
        transcendentals=0,
    )


def add_direct(info, slots, natural, residual, first_tile):
    tile = TILE
    depth, lanes = slots[0][0].shape
    columns = natural.shape[2]
    arrays = [a for pair in slots for a in pair]
    anywhere = pl.BlockSpec(memory_space=pl.ANY)
    block = pl.BlockSpec((tile, columns), lambda i, *_: (first_tile + i, 0))
    operands = [info, *arrays, natural, residual]
    rows = CORES * depth * len(slots)
    return pl.pallas_call(
        functools.partial(direct_kernel, depth),
        grid_spec=pltpu.PrefetchScalarGridSpec(
            num_scalar_prefetch=1,
            grid=(lanes // tile,),
            in_specs=[anywhere] * (len(arrays) + 1) + [block],
            out_specs=block,
            scratch_shapes=[
                pltpu.VMEM((2, rows, tile), natural.dtype),
                pltpu.VMEM((rows, columns), natural.dtype),
                pltpu.SemaphoreType.DMA((2,)),
                pltpu.SemaphoreType.DMA,
            ],
        ),
        out_shape=jax.ShapeDtypeStruct(residual.shape, residual.dtype),
        compiler_params=pltpu.CompilerParams(vmem_limit_bytes=VMEM_BYTES),
        cost_estimate=product_cost(lanes, rows, columns),
    )(*operands)


def whole_kernel(t_ref, v_ref, residual_ref, _, out_ref):
    blocks, depth, tile = t_ref.shape
    out_ref[...] = residual_ref[...] + lax.dot_general(
        t_ref[...].reshape(blocks * depth, tile),
        v_ref[...].reshape(blocks * depth, -1),
        CONTRACT_FIRST,
        preferred_element_type=jnp.float32,
    )


def add_whole(gathered, natural, residual, acc, first_tile):
    tile = TILE
    blocks, depth, lanes = gathered.shape
    columns = natural.shape[2]
    block = pl.BlockSpec((tile, columns), lambda i: (first_tile + i, 0))
    return pl.pallas_call(
        whole_kernel,
        grid=(lanes // tile,),
        in_specs=[
            pl.BlockSpec((blocks, depth, tile), lambda i: (0, 0, i)),
            pl.BlockSpec(natural.shape, lambda i: (0, 0, 0), pipeline_mode=pl.Buffered(1)),
            block,
            pl.BlockSpec(memory_space=pl.ANY),
        ],
        out_specs=block,
        out_shape=jax.ShapeDtypeStruct(residual.shape, residual.dtype),
        input_output_aliases={3: 0},
        compiler_params=pltpu.CompilerParams(vmem_limit_bytes=VMEM_BYTES),
        cost_estimate=product_cost(lanes, blocks * depth, columns),
    )(gathered, natural, residual, acc)


def on_device(chips, row_size, amplitudes, values_stored, irrep_virtual, residual_in):
    occ, depth = amplitudes.shape
    depth_padded = round_up(depth, 16)
    stored_rows = values_stored.shape[0]
    lanes = round_up(occ, TILE)
    edges = [int(edge) for edge in np.cumsum([0, *WHOLE_TILES]) * TILE]

    columns_first = jnp.pad(amplitudes.T, ((0, depth_padded - depth), (0, lanes - occ)))
    chunk = columns_first[:, edges[-1] :]
    got, order, half = gather_integrals(values_stored, row_size)
    blocks = [chunk] + [send_chips(chunk, d, chips) for d in range(1, chips)]
    gathered = [
        lax.all_gather(columns_first[:, left:right], "col", axis=0) for left, right in zip(edges[:-1], edges[1:])
    ]

    pos = stored_positions(irrep_virtual, chips, depth, depth_padded)
    natural = None
    for hops in range(row_size.bit_length()):
        distances = [d for d in got if bin(d).count("1") == hops]
        if not distances:
            continue
        bases = jnp.stack(
            [(lax.axis_index("row") ^ d) * stored_rows for d in distances for _ in got[d]]
        ).astype(jnp.int32)
        natural = add_permuted(pos, [got[d] for d in distances], bases, natural)
        if hops == 1:
            *blocks, natural = lax.optimization_barrier((*blocks, natural))
    slots = [(block, swap_cores(block, chips)) for block in blocks]

    core, chip = lax.axis_index("col") % CORES, lax.axis_index("col") // CORES
    info = jnp.stack([core] + [chip ^ d for d in range(chips)]).astype(jnp.int32)
    acc = add_direct(info, slots, natural, residual_in, edges[-1] // TILE)
    for part, left in zip(gathered, edges):
        acc = add_whole(part, natural, residual_in, acc, left // TILE)
    return acc


def solution(mesh):
    in_specs = (P("row", "col"), P("row", "col"), P(), P("row", "col"))
    out_specs = P("row", "col")
    body = functools.partial(on_device, mesh.shape["col"] // CORES, mesh.shape["row"])
    return jax.shard_map(body, mesh=mesh, in_specs=in_specs, out_specs=out_specs, check_vma=False)
```

```python
import functools

import jax
import jax.numpy as jnp
import numpy as np
from jax import lax
from jax.experimental import pallas as pl
from jax.experimental.pallas import tpu as pltpu
from jax.sharding import PartitionSpec as P

C_SLAB = 2
CORES = 2
TILE = 512
VMEM_BYTES = 58 << 20
CONTRACT_FIRST = (((0,), (0,)), ((), ()))


def round_up(value, step):
    return -(-value // step) * step


def stored_positions(irrep_virtual, chips, depth, depth_padded):
    pair_irrep = jnp.bitwise_xor(irrep_virtual[:C_SLAB][:, None], irrep_virtual[None, :]).reshape(-1)
    count = pair_irrep.shape[0]
    key = pair_irrep * count + jnp.arange(count, dtype=jnp.int32)
    blocks = jnp.pad(
        key.reshape(chips * CORES, depth), ((0, 0), (0, depth_padded - depth)), constant_values=-1
    ).reshape(chips, CORES * depth_padded, 1)
    rank = jnp.sum((key[None, None, :] < blocks).astype(jnp.int32), axis=2, keepdims=True)
    return jnp.where(blocks < 0, -1, rank)


def permute_kernel(groups, has_previous, base_ref, pos_ref, *refs):
    count = sum(len(group) for group in groups)
    joins = sum(len(group) > 1 for group in groups)
    out_ref, token_ref = refs[-2 - joins :][:2]
    joined = list(refs[len(refs) - joins :])
    token_ref[...] = jnp.zeros_like(token_ref)
    total = None
    pos = pos_ref[0]
    for group in groups:
        if len(group) == 1:
            rows_ref = refs[group[0]]
        else:
            rows_ref = joined.pop(0)

            @pl.when(pl.program_id(0) == 0)
            def _(group=group, rows_ref=rows_ref):
                at = 0
                for p in group:
                    rows_ref[at : at + refs[p].shape[0], :] = refs[p][...]
                    at += refs[p].shape[0]

        rows = rows_ref.shape[0]
        picks = pos - base_ref[group[0]] == lax.broadcasted_iota(jnp.int32, (pos.shape[0], rows), 1)
        term = jnp.dot(picks.astype(jnp.bfloat16), rows_ref[...], preferred_element_type=jnp.float32)
        total = term if total is None else total + term
    total = total.astype(out_ref.dtype)
    out_ref[0] = total + refs[count][0] if has_previous else total


def add_permuted(pos, blocks, bases, previous, before):
    chips, rows, _ = pos.shape
    parts = [part for block in blocks for part in block]
    columns = parts[0].shape[1]
    numbers = iter(range(len(parts)))
    groups = tuple(tuple(next(numbers) for _ in block) for block in blocks)
    joined = [
        pltpu.VMEM((sum(part.shape[0] for part in block), columns), parts[0].dtype) for block in blocks if len(block) > 1
    ]
    block_spec = pl.BlockSpec((1, rows, columns), lambda q, *_: (q, 0, 0))
    in_specs = [pl.BlockSpec((1, rows, 1), lambda q, *_: (q, 0, 0))]
    in_specs += [pl.BlockSpec(part.shape, lambda q, *_: (0, 0), pipeline_mode=pl.Buffered(1)) for part in parts]
    operands = [bases, pos, *parts]
    aliases = {}
    if previous is not None:
        in_specs.append(block_spec)
        aliases = {len(operands): 0}
        operands.append(previous)
    in_specs += [pl.BlockSpec(memory_space=pl.ANY)] * len(before)
    operands += before
    return pl.pallas_call(
        functools.partial(permute_kernel, groups, previous is not None),
        grid_spec=pltpu.PrefetchScalarGridSpec(
            num_scalar_prefetch=1, grid=(chips,), in_specs=in_specs,
            out_specs=[block_spec, pl.BlockSpec((8, 128), lambda q, *_: (0, 0))],
            scratch_shapes=joined,
        ),
        out_shape=[
            jax.ShapeDtypeStruct((chips, rows, columns), parts[0].dtype),
            jax.ShapeDtypeStruct((8, 128), jnp.float32),
        ],
        input_output_aliases=aliases,
        compiler_params=pltpu.CompilerParams(vmem_limit_bytes=VMEM_BYTES),
        cost_estimate=pl.CostEstimate(
            flops=2 * chips * rows * columns * sum(part.shape[0] for part in parts),
            bytes_accessed=4 * chips * rows * columns,
            transcendentals=0,
        ),
    )(*operands)


def gather_integrals(values, size):
    half = round_up(values.shape[0] // 2, 16)

    def send(array, bit):
        return lax.ppermute(array, "row", [(i, i ^ bit) for i in range(size)])

    got = {0: [values]}
    order = sorted(range(1, size), key=lambda d: (bin(d).count("1"), d))
    for d in order:
        low, high = d & -d, 1 << (d.bit_length() - 1)
        if low == high:
            got[d] = [send(values, d)]
            continue
        parts = []
        for which, bit in ((0, low), (1, high)):
            source = got[d ^ bit]
            if len(source) == 2:
                piece = source[which]
            else:
                piece = source[0][:half] if which == 0 else source[0][half:]
            parts.append(send(piece, bit))
        got[d] = parts
    return got, order, half


def send_chips(block, moves):
    return lax.ppermute(block, "col", [(z * CORES + core, to * CORES + core) for z, to in moves for core in range(CORES)])


def swap_cores(block, chips):
    return lax.ppermute(block, "col", [(z * CORES + core, z * CORES + 1 - core) for z in chips for core in range(CORES)])


def product_kernel(slots, depth, info_ref, *refs):
    out_ref, buffer, integrals, sems, sem_integrals = refs[-5:]
    n_arrays = CORES * sum(slots)
    arrays, natural_ref, residual_ref = refs[:n_arrays], refs[n_arrays], refs[n_arrays + 1]
    core = info_ref[0]
    tile = residual_ref.shape[0]
    i = pl.program_id(0)

    def fetch(step, half):
        lanes = pl.ds(pl.multiple_of(step * tile, tile), tile)
        at = 0
        for s, slot in enumerate(slots):
            for k in range(slot):

                def start(at=at, s=s):
                    for other in range(CORES):
                        place = (CORES * s + jnp.where(core == other, 0, 1)) * depth
                        pltpu.make_async_copy(
                            arrays[at + other].at[:, lanes],
                            buffer.at[half, pl.ds(pl.multiple_of(place, 16), depth), :],
                            sems.at[half],
                        ).start()

                if slot == 1:
                    start()
                else:
                    pl.when(info_ref[1 + 2 * s] == k)(start)
                at += CORES

    @pl.when(i == 0)
    def _():
        for s in range(len(slots)):
            pltpu.make_async_copy(
                natural_ref.at[info_ref[2 + 2 * s]],
                integrals.at[pl.ds(CORES * depth * s, CORES * depth), :],
                sem_integrals,
            ).start()
        fetch(0, 0)

    @pl.when(i + 1 < pl.num_programs(0))
    def _():
        fetch(i + 1, lax.rem(i + 1, 2))

    @pl.when(i == 0)
    def _():
        pltpu.make_async_copy(integrals, integrals, sem_integrals).wait()

    now = lax.rem(i, 2)
    pltpu.make_async_copy(buffer.at[now], buffer.at[now], sems.at[now]).wait()
    out_ref[...] = residual_ref[...] + lax.dot_general(
        buffer[now], integrals[...], CONTRACT_FIRST, preferred_element_type=jnp.float32
    )


def product_cost(lanes, rows, columns):
    return pl.CostEstimate(
        flops=2 * lanes * columns,
        bytes_accessed=8 * columns,
        transcendentals=0,
    )


def add_product(info, slots, natural, acc, in_place, token):
    tile = TILE
    depth, lanes = slots[0][0][0].shape
    tiles = lanes // tile
    columns = natural.shape[2]
    arrays = [a for slot in slots for pair in slot for a in pair]
    anywhere = pl.BlockSpec(memory_space=pl.ANY)
    block = pl.BlockSpec((tile, columns), lambda i, *_: (i, 0))
    operands = [info, *arrays, natural, acc, token]
    aliases = {len(operands) - 2: 0} if in_place else {}
    rows = CORES * depth * len(slots)
    return pl.pallas_call(
        functools.partial(product_kernel, tuple(len(slot) for slot in slots), depth),
        grid_spec=pltpu.PrefetchScalarGridSpec(
            num_scalar_prefetch=1,
            grid=(tiles,),
            in_specs=[anywhere] * (len(arrays) + 1) + [block, anywhere],
            out_specs=block,
            scratch_shapes=[
                pltpu.VMEM((2, rows, tile), natural.dtype),
                pltpu.VMEM((rows, columns), natural.dtype),
                pltpu.SemaphoreType.DMA((2,)),
                pltpu.SemaphoreType.DMA,
            ],
        ),
        out_shape=jax.ShapeDtypeStruct(acc.shape, acc.dtype),
        input_output_aliases=aliases,
        compiler_params=pltpu.CompilerParams(vmem_limit_bytes=VMEM_BYTES),
        cost_estimate=product_cost(tiles * tile, rows, columns),
    )(*operands)


def on_device(chips, row_size, amplitudes, values_stored, irrep_virtual, residual_in):
    occ, depth = amplitudes.shape
    depth_padded = round_up(depth, 16)
    stored_rows = values_stored.shape[0]
    line = chips == 4
    middle, outward, ends, inner = [(1, 2), (2, 1)], [(1, 0), (2, 3)], [0, 3], [1, 2]

    whole = jnp.pad(amplitudes.T, ((0, depth_padded - depth), (0, round_up(occ, TILE) - occ)))
    a = send_chips(whole, [(z, z ^ 1) for z in range(chips)])
    if line:
        b = send_chips(whole, middle)
    swapped = swap_cores(whole, range(chips))
    got, order, half = gather_integrals(values_stored, row_size)

    pos = stored_positions(irrep_virtual, chips, depth, depth_padded)

    def permuted(distances, previous, before):
        bases = jnp.stack([(lax.axis_index("row") ^ d) * stored_rows for d in distances for _ in got[d]])
        return add_permuted(pos, [got[d] for d in distances], bases.astype(jnp.int32), previous, before)

    near = [d for d in order if bin(d).count("1") == 1]
    far = [d for d in order if bin(d).count("1") > 1]
    natural, token = permuted([0], None, [])
    if line:
        a, b, token = lax.optimization_barrier((a, b, token))
        d = send_chips(a, middle)
        c = send_chips(b, outward)
    if near:
        natural, token = permuted(near, natural, [token] + ([swapped] if line else []))
    if line:
        a, b, d, token = lax.optimization_barrier((a, b, d, token))
        a, b = (a, swap_cores(a, range(chips))), (b, swap_cores(b, inner))
        e = send_chips(d, outward)
        d, c = (d, swap_cores(d, inner)), (c, swap_cores(c, ends))
    for distance in far:
        natural, token = permuted([distance], natural, [token] + ([a[1], b[1], d[1]] if line else []))

    core, chip = lax.axis_index("col") % CORES, lax.axis_index("col") // CORES
    if line:
        at_end = ((chip == 0) | (chip == 3)).astype(jnp.int32)
        left = chip < 2
        info = [core, 0, chip, 0, chip ^ 1, at_end, jnp.where(left, 2, 1), at_end, jnp.where(left, 3, 0)]
        slots = [
            [(whole, swapped)],
            [a],
            [b, c],
        ]
    else:
        blocks = [a] + [send_chips(whole, [(z, z ^ n) for z in range(chips)]) for n in range(2, chips)]
        slots = [[(whole, swapped)]] + [[(block, swap_cores(block, range(chips)))] for block in blocks]
        info = [core] + [number for distance in range(chips) for number in (0, chip ^ distance)]
    info = [jnp.asarray(number, jnp.int32) for number in info]
    early = 1 + 2 * len(slots)
    acc = add_product(jnp.stack(info[:early]), slots, natural, residual_in, False, token)
    if line:
        e, acc = lax.optimization_barrier((e, acc))
        last = [[d, (e, swap_cores(e, ends))]]
        acc = add_product(jnp.stack([core, *info[early:]]), last, natural, acc, True, token)
    return acc


def solution(mesh):
    in_specs = (P("row", "col"), P("row", "col"), P(), P("row", "col"))
    out_specs = P("row", "col")
    body = functools.partial(on_device, mesh.shape["col"] // CORES, mesh.shape["row"])
    return jax.shard_map(body, mesh=mesh, in_specs=in_specs, out_specs=out_specs, check_vma=False)
```

```python
import functools

import jax
import jax.numpy as jnp
import numpy as np
from jax import lax
from jax.experimental import pallas as pl
from jax.experimental.pallas import tpu as pltpu
from jax.sharding import PartitionSpec as P

C_SLAB = 2
CORES = 2
TILE = 512
VMEM_BYTES = 58 << 20
CONTRACT_FIRST = (((0,), (0,)), ((), ()))


def round_up(value, step):
    return -(-value // step) * step


def stored_positions(irrep_virtual, chips, depth, depth_padded):
    pair_irrep = jnp.bitwise_xor(irrep_virtual[:C_SLAB][:, None], irrep_virtual[None, :]).reshape(-1)
    count = pair_irrep.shape[0]
    key = pair_irrep * count + jnp.arange(count, dtype=jnp.int32)
    blocks = jnp.pad(
        key.reshape(chips * CORES, depth), ((0, 0), (0, depth_padded - depth)), constant_values=-1
    ).reshape(chips, CORES * depth_padded, 1)
    rank = jnp.sum((key[None, None, :] < blocks).astype(jnp.int32), axis=2, keepdims=True)
    return jnp.where(blocks < 0, -1, rank)


def permute_kernel(groups, has_previous, base_ref, pos_ref, *refs):
    count = sum(len(group) for group in groups)
    joins = sum(len(group) > 1 for group in groups)
    out_ref, token_ref = refs[-2 - joins :][:2]
    joined = list(refs[len(refs) - joins :])
    token_ref[...] = jnp.zeros_like(token_ref)
    total = None
    pos = pos_ref[0]
    for group in groups:
        if len(group) == 1:
            rows_ref = refs[group[0]]
        else:
            rows_ref = joined.pop(0)

            @pl.when(pl.program_id(0) == 0)
            def _(group=group, rows_ref=rows_ref):
                at = 0
                for p in group:
                    rows_ref[at : at + refs[p].shape[0], :] = refs[p][...]
                    at += refs[p].shape[0]

        rows = rows_ref.shape[0]
        picks = pos - base_ref[group[0]] == lax.broadcasted_iota(jnp.int32, (pos.shape[0], rows), 1)
        term = jnp.dot(picks.astype(jnp.bfloat16), rows_ref[...], preferred_element_type=jnp.float32)
        total = term if total is None else total + term
    total = total.astype(out_ref.dtype)
    out_ref[0] = total + refs[count][0] if has_previous else total


def add_permuted(pos, blocks, bases, previous, before):
    chips, rows, _ = pos.shape
    parts = [part for block in blocks for part in block]
    columns = parts[0].shape[1]
    numbers = iter(range(len(parts)))
    groups = tuple(tuple(next(numbers) for _ in block) for block in blocks)
    joined = [
        pltpu.VMEM((sum(part.shape[0] for part in block), columns), parts[0].dtype) for block in blocks if len(block) > 1
    ]
    block_spec = pl.BlockSpec((1, rows, columns), lambda q, *_: (q, 0, 0))
    in_specs = [pl.BlockSpec((1, rows, 1), lambda q, *_: (q, 0, 0))]
    in_specs += [pl.BlockSpec(part.shape, lambda q, *_: (0, 0), pipeline_mode=pl.Buffered(1)) for part in parts]
    operands = [bases, pos, *parts]
    aliases = {}
    if previous is not None:
        in_specs.append(block_spec)
        aliases = {len(operands): 0}
        operands.append(previous)
    in_specs += [pl.BlockSpec(memory_space=pl.ANY)] * len(before)
    operands += before
    return pl.pallas_call(
        functools.partial(permute_kernel, groups, previous is not None),
        grid_spec=pltpu.PrefetchScalarGridSpec(
            num_scalar_prefetch=1, grid=(chips,), in_specs=in_specs,
            out_specs=[block_spec, pl.BlockSpec((8, 128), lambda q, *_: (0, 0))],
            scratch_shapes=joined,
        ),
        out_shape=[
            jax.ShapeDtypeStruct((chips, rows, columns), parts[0].dtype),
            jax.ShapeDtypeStruct((8, 128), jnp.float32),
        ],
        input_output_aliases=aliases,
        compiler_params=pltpu.CompilerParams(vmem_limit_bytes=VMEM_BYTES),
        cost_estimate=pl.CostEstimate(
            flops=2 * chips * rows * columns * sum(part.shape[0] for part in parts),
            bytes_accessed=4 * chips * rows * columns,
            transcendentals=0,
        ),
    )(*operands)


def gather_integrals(values, size):
    half = round_up(values.shape[0] // 2, 16)

    def send(array, bit):
        return lax.ppermute(array, "row", [(i, i ^ bit) for i in range(size)])

    got = {0: [values]}
    order = sorted(range(1, size), key=lambda d: (bin(d).count("1"), d))
    for d in order:
        low, high = d & -d, 1 << (d.bit_length() - 1)
        if low == high:
            got[d] = [send(values, d)]
            continue
        parts = []
        for which, bit in ((0, low), (1, high)):
            source = got[d ^ bit]
            if len(source) == 2:
                piece = source[which]
            else:
                piece = source[0][:half] if which == 0 else source[0][half:]
            parts.append(send(piece, bit))
        got[d] = parts
    return got, order, half


def send_chips(block, moves):
    return lax.ppermute(block, "col", [(z * CORES + core, to * CORES + core) for z, to in moves for core in range(CORES)])


def swap_cores(block, chips):
    return lax.ppermute(block, "col", [(z * CORES + core, z * CORES + 1 - core) for z in chips for core in range(CORES)])


def product_kernel(slots, chips, depth, halves, info_ref, *refs):
    joined_ref, buffer, integrals, sems, sems_integrals = refs[-5:]
    out_ref, far_ref = refs[-7:-5]
    count = len(slots)
    n_arrays = CORES * sum(slots)
    arrays = refs[:n_arrays]
    natural_ref, residual_ref, pos_ref = refs[n_arrays : n_arrays + 3]
    missing = refs[n_arrays + 3 : n_arrays + 3 + halves]
    core = info_ref[0]
    tile = residual_ref.shape[0]
    i = pl.program_id(0)

    def fetch(step, half):
        lanes = pl.ds(pl.multiple_of(step * tile, tile), tile)
        at = 0
        for s, slot in enumerate(slots):
            for k in range(slot):

                def start(at=at, s=s):
                    for other in range(CORES):
                        place = (CORES * s + jnp.where(core == other, 0, 1)) * depth
                        pltpu.make_async_copy(
                            arrays[at + other].at[:, lanes],
                            buffer.at[half, pl.ds(pl.multiple_of(place, 16), depth), :],
                            sems.at[half],
                        ).start()

                if slot == 1:
                    start()
                else:
                    pl.when(info_ref[1 + 2 * s] == k)(start)
                at += CORES

    def copy_integrals(q):
        return pltpu.make_async_copy(natural_ref.at[q], integrals.at[q], sems_integrals.at[q])

    @pl.when(i == 0)
    def _():
        for q in range(chips):
            copy_integrals(q).start()
        fetch(0, 0)

    @pl.when(i + 1 < pl.num_programs(0))
    def _():
        fetch(i + 1, lax.rem(i + 1, 2))

    @pl.when(i == 0)
    def _():
        at = 0
        for part in missing:
            joined_ref[at : at + part.shape[0], :] = part[...]
            at += part.shape[0]
        for q in range(chips):
            rows = joined_ref.shape[0]
            picks = pos_ref[q] - info_ref[2 + 2 * count] == lax.broadcasted_iota(
                jnp.int32, (pos_ref.shape[1], rows), 1
            )
            term = jnp.dot(picks.astype(jnp.bfloat16), joined_ref[...], preferred_element_type=jnp.float32)
            copy_integrals(q).wait()
            integrals[q] = integrals[q] + term.astype(integrals.dtype)
        far_ref[...] = integrals[info_ref[1 + 2 * count]]

    now = lax.rem(i, 2)
    pltpu.make_async_copy(buffer.at[now], buffer.at[now], sems.at[now]).wait()
    total = residual_ref[...]
    for s in range(count):
        total += lax.dot_general(
            buffer[now, CORES * depth * s : CORES * depth * (s + 1), :],
            integrals[info_ref[2 + 2 * s]],
            CONTRACT_FIRST,
            preferred_element_type=jnp.float32,
        )
    out_ref[...] = total


def last_kernel(mine, info_ref, *refs):
    arrays, (far_ref, acc_ref, out_ref, buffer, sem) = refs[:-5], refs[-5:]
    depth, tile = arrays[0].shape[0], acc_ref.shape[0]
    i = pl.program_id(0)

    def fetch(step, half):
        lanes = pl.ds(pl.multiple_of(step * tile, tile), tile)
        for k in range(mine):

            @pl.when(info_ref[1] == k)
            def _(k=k):
                for other in range(CORES):
                    place = jnp.where(info_ref[0] == other, 0, depth)
                    pltpu.make_async_copy(
                        arrays[CORES * k + other].at[:, lanes],
                        buffer.at[half, pl.ds(pl.multiple_of(place, 16), depth), :],
                        sem.at[half],
                    ).start()

    @pl.when(i == 0)
    def _():
        fetch(0, 0)

    @pl.when(i + 1 < pl.num_programs(0))
    def _():
        fetch(i + 1, lax.rem(i + 1, 2))

    now = lax.rem(i, 2)
    pltpu.make_async_copy(buffer.at[now], buffer.at[now], sem.at[now]).wait()
    out_ref[...] = acc_ref[...] + lax.dot_general(
        buffer[now], far_ref[...], CONTRACT_FIRST, preferred_element_type=jnp.float32
    )


def product_cost(lanes, rows, columns):
    return pl.CostEstimate(
        flops=2 * lanes * columns,
        bytes_accessed=8 * columns,
        transcendentals=0,
    )


def add_product(info, slots, natural, pos, missing, acc, before):
    tile = TILE
    depth, lanes = slots[0][0][0].shape
    chips, chip_rows, columns = natural.shape
    arrays = [a for slot in slots for pair in slot for a in pair]
    anywhere = pl.BlockSpec(memory_space=pl.ANY)
    block = pl.BlockSpec((tile, columns), lambda i, *_: (i, 0))
    rows = CORES * depth * len(slots)

    def once(shape):
        return pl.BlockSpec(shape, lambda i, *_: (0,) * len(shape), pipeline_mode=pl.Buffered(1))

    return pl.pallas_call(
        functools.partial(product_kernel, tuple(len(slot) for slot in slots), chips, depth, len(missing)),
        grid_spec=pltpu.PrefetchScalarGridSpec(
            num_scalar_prefetch=1,
            grid=(lanes // tile,),
            in_specs=[anywhere] * (len(arrays) + 1) + [block, once(pos.shape)] + [once(part.shape) for part in missing] + [anywhere] * len(before),
            out_specs=[block, pl.BlockSpec((chip_rows, columns), lambda i, *_: (0, 0))],
            scratch_shapes=[
                pltpu.VMEM((sum(part.shape[0] for part in missing), columns), natural.dtype),
                pltpu.VMEM((2, rows, tile), natural.dtype),
                pltpu.VMEM(natural.shape, natural.dtype),
                pltpu.SemaphoreType.DMA((2,)),
                pltpu.SemaphoreType.DMA((chips,)),
            ],
        ),
        out_shape=[
            jax.ShapeDtypeStruct(acc.shape, acc.dtype),
            jax.ShapeDtypeStruct((chip_rows, columns), natural.dtype),
        ],
        compiler_params=pltpu.CompilerParams(vmem_limit_bytes=VMEM_BYTES),
        cost_estimate=product_cost(lanes, rows, columns),
    )(info, *arrays, natural, acc, pos, *missing, *before)


def add_last(info, slot, far, acc):
    tile = TILE
    depth, lanes = slot[0][0].shape
    arrays = [a for pair in slot for a in pair]
    block = pl.BlockSpec((tile, far.shape[1]), lambda i, *_: (i, 0))
    operands = [info, *arrays, far, acc]
    return pl.pallas_call(
        functools.partial(last_kernel, len(slot)),
        grid_spec=pltpu.PrefetchScalarGridSpec(
            num_scalar_prefetch=1,
            grid=(lanes // tile,),
            in_specs=[pl.BlockSpec(memory_space=pl.ANY)] * len(arrays)
            + [pl.BlockSpec(far.shape, lambda i, *_: (0, 0), pipeline_mode=pl.Buffered(1)), block],
            out_specs=block,
            scratch_shapes=[pltpu.VMEM((2, CORES * depth, tile), far.dtype), pltpu.SemaphoreType.DMA((2,))],
        ),
        out_shape=jax.ShapeDtypeStruct(acc.shape, acc.dtype),
        input_output_aliases={len(operands) - 1: 0},
        compiler_params=pltpu.CompilerParams(vmem_limit_bytes=VMEM_BYTES),
        cost_estimate=product_cost(lanes, CORES * depth, far.shape[1]),
    )(*operands)


def on_device(chips, row_size, amplitudes, values_stored, irrep_virtual, residual_in):
    occ, depth = amplitudes.shape
    depth_padded = round_up(depth, 16)
    stored_rows = values_stored.shape[0]
    line = chips == 4
    middle, outward, ends, inner = [(1, 2), (2, 1)], [(1, 0), (2, 3)], [0, 3], [1, 2]

    whole = jnp.pad(amplitudes.T, ((0, depth_padded - depth), (0, round_up(occ, TILE) - occ)))
    a = send_chips(whole, [(z, z ^ 1) for z in range(chips)])
    if line:
        b = send_chips(whole, middle)
    swapped = swap_cores(whole, range(chips))
    got, order, half = gather_integrals(values_stored, row_size)

    pos = stored_positions(irrep_virtual, chips, depth, depth_padded)

    def permuted(distances, previous, before):
        bases = jnp.stack([(lax.axis_index("row") ^ d) * stored_rows for d in distances for _ in got[d]])
        return add_permuted(pos, [got[d] for d in distances], bases.astype(jnp.int32), previous, before)

    near = [d for d in order if bin(d).count("1") == 1]
    far = [d for d in order if bin(d).count("1") > 1]
    natural, token = permuted([0], None, [])
    if line:
        a, b, token = lax.optimization_barrier((a, b, token))
        d = send_chips(a, middle)
        c = send_chips(b, outward)
    if near:
        natural, token = permuted(near, natural, [token] + ([swapped] if line else []))
    if line:
        a, b, d, token = lax.optimization_barrier((a, b, d, token))
        a, b = (a, swap_cores(a, range(chips))), (b, swap_cores(b, inner))
        e = send_chips(d, outward)
        d, c = (d, swap_cores(d, inner)), (c, swap_cores(c, ends))
    for distance in far[:-1]:
        natural, token = permuted([distance], natural, [token])
    missing, missing_at = got[far[-1]], (lax.axis_index("row") ^ far[-1]) * stored_rows

    core, chip = lax.axis_index("col") % CORES, lax.axis_index("col") // CORES
    if line:
        at_end = ((chip == 0) | (chip == 3)).astype(jnp.int32)
        left = chip < 2
        info = [core, 0, chip, 0, chip ^ 1, at_end, jnp.where(left, 2, 1), at_end, jnp.where(left, 3, 0)]
        slots = [
            [(whole, swapped)],
            [a],
            [b, c],
        ]
    else:
        blocks = [a] + [send_chips(whole, [(z, z ^ n) for z in range(chips)]) for n in range(2, chips)]
        slots = [[(whole, swapped)]] + [[(block, swap_cores(block, range(chips)))] for block in blocks]
        info = [core] + [number for distance in range(chips) for number in (0, chip ^ distance)]
    info = [jnp.asarray(number, jnp.int32) for number in [*info, missing_at]]
    if not line:
        return add_product(jnp.stack([*info[:-1], info[0], info[-1]]), slots, natural, pos, missing, residual_in, [token])[0]
    choice, far_chip = info[-3], info[-2]
    acc, far_rows = add_product(
        jnp.stack([*info[:-3], far_chip, info[-1]]), slots, natural, pos, missing, residual_in, [token, d[1]]
    )
    e, acc = lax.optimization_barrier((e, acc))
    e = (e, swap_cores(e, ends))
    return add_last(jnp.stack([core, choice]), [d, e], far_rows, acc)


def solution(mesh):
    in_specs = (P("row", "col"), P("row", "col"), P(), P("row", "col"))
    out_specs = P("row", "col")
    body = functools.partial(on_device, mesh.shape["col"] // CORES, mesh.shape["row"])
    return jax.shard_map(body, mesh=mesh, in_specs=in_specs, out_specs=out_specs, check_vma=False)
```

```python
import functools

import jax
import jax.numpy as jnp
import numpy as np
from jax import lax
from jax.experimental import pallas as pl
from jax.experimental.pallas import tpu as pltpu
from jax.sharding import PartitionSpec as P

C_SLAB = 2
CORES = 2
TILE = 512
VMEM_BYTES = 58 << 20
CONTRACT_FIRST = (((0,), (0,)), ((), ()))


def round_up(value, step):
    return -(-value // step) * step


def stored_positions(irrep_virtual, chips, depth, depth_padded):
    pair_irrep = jnp.bitwise_xor(irrep_virtual[:C_SLAB][:, None], irrep_virtual[None, :]).reshape(-1)
    count = pair_irrep.shape[0]
    key = pair_irrep * count + jnp.arange(count, dtype=jnp.int32)
    blocks = jnp.pad(
        key.reshape(chips * CORES, depth), ((0, 0), (0, depth_padded - depth)), constant_values=-1
    ).reshape(chips, CORES * depth_padded, 1)
    rank = jnp.sum((key[None, None, :] < blocks).astype(jnp.int32), axis=2, keepdims=True)
    return jnp.where(blocks < 0, -1, rank)


def permute_kernel(groups, has_previous, base_ref, pos_ref, *refs):
    count = sum(len(group) for group in groups)
    joins = sum(len(group) > 1 for group in groups)
    out_ref, token_ref = refs[-2 - joins :][:2]
    joined = list(refs[len(refs) - joins :])
    token_ref[...] = jnp.zeros_like(token_ref)
    total = None
    pos = pos_ref[0]
    for group in groups:
        if len(group) == 1:
            rows_ref = refs[group[0]]
        else:
            rows_ref = joined.pop(0)

            @pl.when(pl.program_id(0) == 0)
            def _(group=group, rows_ref=rows_ref):
                at = 0
                for p in group:
                    rows_ref[at : at + refs[p].shape[0], :] = refs[p][...]
                    at += refs[p].shape[0]

        rows = rows_ref.shape[0]
        picks = pos - base_ref[group[0]] == lax.broadcasted_iota(jnp.int32, (pos.shape[0], rows), 1)
        term = jnp.dot(picks.astype(jnp.bfloat16), rows_ref[...], preferred_element_type=jnp.float32)
        total = term if total is None else total + term
    total = total.astype(out_ref.dtype)
    out_ref[0] = total + refs[count][0] if has_previous else total


def add_permuted(pos, blocks, bases, previous, before):
    chips, rows, _ = pos.shape
    parts = [part for block in blocks for part in block]
    columns = parts[0].shape[1]
    numbers = iter(range(len(parts)))
    groups = tuple(tuple(next(numbers) for _ in block) for block in blocks)
    joined = [
        pltpu.VMEM((sum(part.shape[0] for part in block), columns), parts[0].dtype) for block in blocks if len(block) > 1
    ]
    block_spec = pl.BlockSpec((1, rows, columns), lambda q, *_: (q, 0, 0))
    in_specs = [pl.BlockSpec((1, rows, 1), lambda q, *_: (q, 0, 0))]
    in_specs += [pl.BlockSpec(part.shape, lambda q, *_: (0, 0), pipeline_mode=pl.Buffered(1)) for part in parts]
    operands = [bases, pos, *parts]
    aliases = {}
    if previous is not None:
        in_specs.append(block_spec)
        aliases = {len(operands): 0}
        operands.append(previous)
    in_specs += [pl.BlockSpec(memory_space=pl.ANY)] * len(before)
    operands += before
    return pl.pallas_call(
        functools.partial(permute_kernel, groups, previous is not None),
        grid_spec=pltpu.PrefetchScalarGridSpec(
            num_scalar_prefetch=1, grid=(chips,), in_specs=in_specs,
            out_specs=[block_spec, pl.BlockSpec((8, 128), lambda q, *_: (0, 0))],
            scratch_shapes=joined,
        ),
        out_shape=[
            jax.ShapeDtypeStruct((chips, rows, columns), parts[0].dtype),
            jax.ShapeDtypeStruct((8, 128), jnp.float32),
        ],
        input_output_aliases=aliases,
        compiler_params=pltpu.CompilerParams(vmem_limit_bytes=VMEM_BYTES),
        cost_estimate=pl.CostEstimate(
            flops=2 * chips * rows * columns * sum(part.shape[0] for part in parts),
            bytes_accessed=4 * chips * rows * columns,
            transcendentals=0,
        ),
    )(*operands)


def gather_integrals(values, size):
    half = round_up(values.shape[0] // 2, 16)

    def send(array, bit):
        return lax.ppermute(array, "row", [(i, i ^ bit) for i in range(size)])

    got = {0: [values]}
    order = sorted(range(1, size), key=lambda d: (bin(d).count("1"), d))
    for d in order:
        low, high = d & -d, 1 << (d.bit_length() - 1)
        if low == high:
            got[d] = [send(values, d)]
            continue
        parts = []
        for which, bit in ((0, low), (1, high)):
            source = got[d ^ bit]
            if len(source) == 2:
                piece = source[which]
            else:
                piece = source[0][:half] if which == 0 else source[0][half:]
            parts.append(send(piece, bit))
        got[d] = parts
    return got, order, half


def send_chips(block, moves):
    return lax.ppermute(block, "col", [(z * CORES + core, to * CORES + core) for z, to in moves for core in range(CORES)])


def swap_cores(block, chips):
    return lax.ppermute(block, "col", [(z * CORES + core, z * CORES + 1 - core) for z in chips for core in range(CORES)])


def product_kernel(slots, chips, depth, halves, info_ref, *refs):
    joined_ref, buffer, integrals, sems, sems_integrals = refs[-5:]
    out_ref, far_ref = refs[-7:-5]
    count = len(slots)
    n_arrays = CORES * sum(slots)
    arrays = refs[:n_arrays]
    natural_ref, residual_ref, pos_ref = refs[n_arrays : n_arrays + 3]
    missing = refs[n_arrays + 3 : n_arrays + 3 + halves]
    core = info_ref[0]
    tile = residual_ref.shape[0]
    i = pl.program_id(0)

    def fetch(step, half):
        lanes = pl.ds(pl.multiple_of(step * tile, tile), tile)
        at = 0
        for s, slot in enumerate(slots):
            for k in range(slot):

                def start(at=at, s=s):
                    for other in range(CORES):
                        place = (CORES * s + jnp.where(core == other, 0, 1)) * depth
                        pltpu.make_async_copy(
                            arrays[at + other].at[:, lanes],
                            buffer.at[half, pl.ds(pl.multiple_of(place, 16), depth), :],
                            sems.at[half],
                        ).start()

                if slot == 1:
                    start()
                else:
                    pl.when(info_ref[1 + 2 * s] == k)(start)
                at += CORES

    def copy_integrals(q):
        return pltpu.make_async_copy(natural_ref.at[q], integrals.at[q], sems_integrals.at[q])

    @pl.when(i == 0)
    def _():
        for q in range(chips):
            copy_integrals(q).start()
        fetch(0, 0)

    @pl.when(i + 1 < pl.num_programs(0))
    def _():
        fetch(i + 1, lax.rem(i + 1, 2))

    @pl.when(i == 0)
    def _():
        at = 0
        for part in missing:
            joined_ref[at : at + part.shape[0], :] = part[...]
            at += part.shape[0]
        for q in range(chips):
            rows = joined_ref.shape[0]
            picks = pos_ref[q] - info_ref[2 + 2 * count] == lax.broadcasted_iota(
                jnp.int32, (pos_ref.shape[1], rows), 1
            )
            term = jnp.dot(picks.astype(jnp.bfloat16), joined_ref[...], preferred_element_type=jnp.float32)
            copy_integrals(q).wait()
            integrals[q] = integrals[q] + term.astype(integrals.dtype)
        far_ref[...] = integrals[info_ref[1 + 2 * count]]

    now = lax.rem(i, 2)
    pltpu.make_async_copy(buffer.at[now], buffer.at[now], sems.at[now]).wait()
    total = residual_ref[...]
    for s in range(count):
        total += lax.dot_general(
            buffer[now, CORES * depth * s : CORES * depth * (s + 1), :],
            integrals[info_ref[2 + 2 * s]],
            CONTRACT_FIRST,
            preferred_element_type=jnp.float32,
        )
    out_ref[...] = total


def last_kernel(mine, info_ref, *refs):
    arrays, (far_ref, acc_ref, out_ref, buffer, sem) = refs[:-5], refs[-5:]
    depth, tile = arrays[0].shape[0], acc_ref.shape[0]
    i = pl.program_id(0)

    def fetch(step, half):
        lanes = pl.ds(pl.multiple_of(step * tile, tile), tile)
        for k in range(mine):

            @pl.when(info_ref[info_ref.shape[0] - 1] == k)
            def _(k=k):
                for other in range(CORES):
                    place = jnp.where(info_ref[0] == other, 0, depth)
                    pltpu.make_async_copy(
                        arrays[CORES * k + other].at[:, lanes],
                        buffer.at[half, pl.ds(pl.multiple_of(place, 16), depth), :],
                        sem.at[half],
                    ).start()

    @pl.when(i == 0)
    def _():
        fetch(0, 0)

    @pl.when(i + 1 < pl.num_programs(0))
    def _():
        fetch(i + 1, lax.rem(i + 1, 2))

    now = lax.rem(i, 2)
    pltpu.make_async_copy(buffer.at[now], buffer.at[now], sem.at[now]).wait()
    out_ref[...] = acc_ref[...] + lax.dot_general(
        buffer[now], far_ref[...], CONTRACT_FIRST, preferred_element_type=jnp.float32
    )


def product_cost(lanes, rows, columns):
    return pl.CostEstimate(
        flops=2 * lanes * columns,
        bytes_accessed=8 * columns,
        transcendentals=0,
    )


def add_product(info, slots, natural, pos, missing, acc, before):
    tile = TILE // 2
    depth, lanes = slots[0][0][0].shape
    chips, chip_rows, columns = natural.shape
    arrays = [a for slot in slots for pair in slot for a in pair]
    anywhere = pl.BlockSpec(memory_space=pl.ANY)
    block = pl.BlockSpec((tile, columns), lambda i, *_: (i, 0))
    rows = CORES * depth * len(slots)

    def once(shape):
        return pl.BlockSpec(shape, lambda i, *_: (0,) * len(shape), pipeline_mode=pl.Buffered(1))

    return pl.pallas_call(
        functools.partial(product_kernel, tuple(len(slot) for slot in slots), chips, depth, len(missing)),
        grid_spec=pltpu.PrefetchScalarGridSpec(
            num_scalar_prefetch=1,
            grid=(lanes // tile,),
            in_specs=[anywhere] * (len(arrays) + 1) + [block, once(pos.shape)] + [once(part.shape) for part in missing] + [anywhere] * len(before),
            out_specs=[block, pl.BlockSpec((chip_rows, columns), lambda i, *_: (0, 0))],
            scratch_shapes=[
                pltpu.VMEM((sum(part.shape[0] for part in missing), columns), natural.dtype),
                pltpu.VMEM((2, rows, tile), natural.dtype),
                pltpu.VMEM(natural.shape, natural.dtype),
                pltpu.SemaphoreType.DMA((2,)),
                pltpu.SemaphoreType.DMA((chips,)),
            ],
        ),
        out_shape=[
            jax.ShapeDtypeStruct(acc.shape, acc.dtype),
            jax.ShapeDtypeStruct((chip_rows, columns), natural.dtype),
        ],
        compiler_params=pltpu.CompilerParams(vmem_limit_bytes=VMEM_BYTES),
        cost_estimate=product_cost(lanes, rows, columns),
    )(info, *arrays, natural, acc, pos, *missing, *before)


def add_last(info, slot, far, acc):
    tile = TILE
    depth, lanes = slot[0][0].shape
    arrays = [a for pair in slot for a in pair]
    block = pl.BlockSpec((tile, far.shape[1]), lambda i, *_: (i, 0))
    operands = [info, *arrays, far, acc]
    return pl.pallas_call(
        functools.partial(last_kernel, len(slot)),
        grid_spec=pltpu.PrefetchScalarGridSpec(
            num_scalar_prefetch=1,
            grid=(lanes // tile,),
            in_specs=[pl.BlockSpec(memory_space=pl.ANY)] * len(arrays)
            + [pl.BlockSpec(far.shape, lambda i, *_: (0, 0), pipeline_mode=pl.Buffered(1)), block],
            out_specs=block,
            scratch_shapes=[pltpu.VMEM((2, CORES * depth, tile), far.dtype), pltpu.SemaphoreType.DMA((2,))],
        ),
        out_shape=jax.ShapeDtypeStruct(acc.shape, acc.dtype),
        input_output_aliases={len(operands) - 1: 0},
        compiler_params=pltpu.CompilerParams(vmem_limit_bytes=VMEM_BYTES),
        cost_estimate=product_cost(lanes, CORES * depth, far.shape[1]),
    )(*operands)


def on_device(chips, row_size, amplitudes, values_stored, irrep_virtual, residual_in):
    occ, depth = amplitudes.shape
    depth_padded = round_up(depth, 16)
    stored_rows = values_stored.shape[0]
    line = chips == 4
    middle, outward, ends, inner = [(1, 2), (2, 1)], [(1, 0), (2, 3)], [0, 3], [1, 2]

    whole = jnp.pad(amplitudes.T, ((0, depth_padded - depth), (0, round_up(occ, TILE) - occ)))
    a = send_chips(whole, [(z, z ^ 1) for z in range(chips)])
    if line:
        b = send_chips(whole, middle)
    swapped = swap_cores(whole, range(chips))
    got, order, half = gather_integrals(values_stored, row_size)

    pos = stored_positions(irrep_virtual, chips, depth, depth_padded)

    def permuted(distances, previous, before):
        bases = jnp.stack([(lax.axis_index("row") ^ d) * stored_rows for d in distances for _ in got[d]])
        return add_permuted(pos, [got[d] for d in distances], bases.astype(jnp.int32), previous, before)

    near = [d for d in order if bin(d).count("1") == 1]
    far = [d for d in order if bin(d).count("1") > 1]
    natural, token = permuted([0], None, [])
    if line:
        a, b, token = lax.optimization_barrier((a, b, token))
        d = send_chips(a, middle)
        c = send_chips(b, outward)
    if near:
        natural, token = permuted(near, natural, [token] + ([swapped] if line else []))
    if line:
        a, b, d, token = lax.optimization_barrier((a, b, d, token))
        a, b = (a, swap_cores(a, range(chips))), (b, swap_cores(b, inner))
        e = send_chips(d, outward)
        d, c = (d, swap_cores(d, inner)), (c, swap_cores(c, ends))
    for distance in far[:-1]:
        natural, token = permuted([distance], natural, [token])
    missing, missing_at = got[far[-1]], (lax.axis_index("row") ^ far[-1]) * stored_rows

    core, chip = lax.axis_index("col") % CORES, lax.axis_index("col") // CORES
    if line:
        at_end = ((chip == 0) | (chip == 3)).astype(jnp.int32)
        left = chip < 2
        info = [core, 0, chip, 0, chip ^ 1, at_end, jnp.where(left, 2, 1), at_end, jnp.where(left, 3, 0)]
        slots = [
            [(whole, swapped)],
            [a],
            [b, c],
        ]
    else:
        blocks = [a] + [send_chips(whole, [(z, z ^ n) for z in range(chips)]) for n in range(2, chips)]
        slots = [[(whole, swapped)]] + [[(block, swap_cores(block, range(chips)))] for block in blocks]
        info = [core] + [number for distance in range(chips) for number in (0, chip ^ distance)]
    info = [jnp.asarray(number, jnp.int32) for number in [*info, missing_at]]
    if not line:
        return add_product(jnp.stack([*info[:-1], info[0], info[-1]]), slots, natural, pos, missing, residual_in, [token])[0]
    choice, far_chip = info[-3], info[-2]
    info = jnp.stack([*info[:-3], far_chip, info[-1], choice])
    acc, far_rows = add_product(
        info, slots, natural, pos, missing, residual_in, [token, d[1]]
    )
    e, acc = lax.optimization_barrier((e, acc))
    e = (e, swap_cores(e, ends))
    return add_last(info, [d, e], far_rows, acc)


def solution(mesh):
    in_specs = (P("row", "col"), P("row", "col"), P(), P("row", "col"))
    out_specs = P("row", "col")
    body = functools.partial(on_device, mesh.shape["col"] // CORES, mesh.shape["row"])
    return jax.shard_map(body, mesh=mesh, in_specs=in_specs, out_specs=out_specs, check_vma=False)
```
